128 devices in a mesh: dp: 8 (over y_lo, z), tensor: 16 (over x, y_hi, core).
Axes of the slice: x: 4, y: 4 (y_hi: 2, y_lo: 2; y = y_hi * 2 + y_lo), z: 4, core: 2. Of those that a mesh axis runs over, the one named last changes fastest.
Arguments:
- acts: bfloat16 [8192, 8192], P('dp', 'tensor'), may hold values from -1.265625 to 1.265625, as said below
- grad_out: bfloat16 [8192, 6144], P(('dp', 'tensor')), may hold values from -6 to 6
- weight: bfloat16 [8192, 6144], P('tensor'), may hold values from -0.078125 to 0.078125
- residue: bfloat16 [8, 8192, 6144], P('dp', 'tensor'), may hold values from -40 to 40, as said below
- start_q: float32 [6144, 32], replicated, may hold values from -6 to 6
Outputs:
- grad_in: bfloat16 [8192, 8192], P('dp', 'tensor')
- p_factor: float32 [8192, 32], P('tensor')
- q_factor: float32 [6144, 32], replicated
- new_residue: bfloat16 [8, 8192, 6144], P('dp', 'tensor')
The draws below stay inside these ranges and needn't reach their ends.
Inputs may be any that keep to these rules, and one draw needn't show every extreme that they name: `acts`: activations with feature scales that differ by column. `residue`: error memory with row and column scales that differ.
All inputs are finite; a program needn't handle non-finite values.
Results may differ from the reference program's by a relative error of at most 0.00055.
Values may be sent and summed in bfloat16 or wider, within the bound.
A program may use at most 128 MiB of HBM per device.

```python
import jax
import jax.numpy as jnp
from jax import lax

D_IN = 8192
D_OUT = 6144
RANK = 32
TOK_REP = 1024
REPLICAS = 8
TOKENS = 8192


def draw_acts(key, part):
    key = jax.random.fold_in(key, 11)
    key_scale, key_main = jax.random.split(key, 2)
    position = jnp.arange(D_IN, dtype=jnp.float32) / D_IN
    rough = jax.random.uniform(key_scale, (D_IN,), jnp.float32)
    column_scale = jnp.exp(jnp.log(10.0) * (0.5 * position + 0.5 * rough))
    divisor = float(TOK_REP) ** 0.5
    main = jnp.clip(jax.random.normal(key_main, (TOKENS, D_IN), jnp.float32), -4.0, 4.0)
    values = main * column_scale / divisor
    return values.astype(jnp.bfloat16)


def draw_residue(key, part):
    key = jax.random.fold_in(key, 23)
    key_rows, key_cols, key_main = jax.random.split(key, 3)
    position = jnp.arange(D_IN, dtype=jnp.float32) / D_IN
    row_rough = jax.random.uniform(key_rows, (1, D_IN, 1), jnp.float32)
    row_scale = jnp.exp(jnp.log(10.0) * (0.5 * position[None, :, None] + 0.5 * row_rough))
    col_scale = jnp.exp(0.5 * jnp.log(10.0) * jax.random.uniform(key_cols, (1, 1, D_OUT), jnp.float32))
    main = jnp.clip(jax.random.normal(key_main, (REPLICAS, D_IN, D_OUT), jnp.float32), -4.0, 4.0)
    return (main * row_scale * col_scale / 4.0).astype(jnp.bfloat16)


def block_levels(rng, extent, pieces, low, top_value):
    factor_of, own = 1.0, jax.random.fold_in(rng, 6)
    for axis_at, parts in pieces:
        draws = jnp.exp(jax.random.uniform(jax.random.fold_in(own, axis_at), (parts,), jnp.float32, low / len(pieces), top_value / len(pieces)))
        factor_of = factor_of * jnp.repeat(draws, extent[axis_at] // parts).reshape([-1 if axis == axis_at else 1 for axis in range(len(extent))])
    return factor_of


def normal_values(stream_key, extent, spread, reach, cuts=(), kind=jnp.bfloat16):
    drawn = spread * jax.random.normal(stream_key, extent, jnp.float32)
    if cuts:
        drawn = drawn * block_levels(stream_key, extent, cuts, -0.22, 0.18)
    return jnp.clip(drawn, -reach, reach).astype(kind)


def setup_inputs(seed: int = 0) -> dict:
    streams_of = jax.random.split(jax.random.key(seed), 6)
    return {
        "acts": draw_acts(jax.random.fold_in(streams_of[5], 71), 0),
        "grad_out": normal_values(streams_of[1], (TOKENS, D_OUT), 1.0, 6.0, ((0, 128),)),
        "weight": normal_values(streams_of[2], (D_IN, D_OUT), D_OUT ** -0.5, 0.078125, ((0, 16),)),
        "residue": draw_residue(jax.random.fold_in(streams_of[5], 71), 0),
        "start_q": normal_values(streams_of[4], (D_OUT, RANK), 1.0, 6.0, (), jnp.float32),
    }


def reference(acts, grad_out, weight, residue, start_q):
    highest = lax.Precision.HIGHEST
    grad_in = lax.dot_general(grad_out.astype(jnp.float32), weight.astype(jnp.float32), (((1,), (1,)), ((), ())), preferred_element_type=jnp.float32).astype(jnp.bfloat16)
    merged_list = []
    sketch = jnp.zeros((D_IN, RANK), jnp.float32)
    for replica in range(REPLICAS):
        rows_a = acts[replica * TOK_REP:(replica + 1) * TOK_REP]
        rows_g = grad_out[replica * TOK_REP:(replica + 1) * TOK_REP]
        wgrad = lax.dot_general(rows_a.astype(jnp.float32), rows_g.astype(jnp.float32), (((0,), (0,)), ((), ())), preferred_element_type=jnp.float32)
        merged = wgrad + residue[replica].astype(jnp.float32)
        merged_list.append(merged)
        sketch = sketch + jnp.dot(merged, start_q, precision=highest)
    sketch = sketch / REPLICAS
    gram = jnp.dot(sketch.T, sketch, precision=highest) / D_IN
    lower_factor = jnp.linalg.cholesky(gram)
    p_factor = jax.scipy.linalg.solve_triangular(lower_factor, sketch.T, lower=True).T
    q_total = jnp.zeros((D_OUT, RANK), jnp.float32)
    for replica in range(REPLICAS):
        q_total = q_total + jnp.dot(merged_list[replica].T, p_factor, precision=highest)
    scale_root = float(D_IN) ** 0.5
    q_factor = q_total / (REPLICAS * scale_root)
    approx = jnp.dot(p_factor, q_factor.T, precision=highest) / scale_root
    new_residue = jnp.stack([(merged_list[replica] - approx).astype(jnp.bfloat16) for replica in range(REPLICAS)])
    return (grad_in, p_factor, q_factor, new_residue)
```

```python
import math

import jax
import jax.numpy as jnp
from jax import lax
from jax.experimental import pallas as pl
from jax.experimental.pallas import tpu as pltpu
from jax.sharding import PartitionSpec as P

MESH = pl.DeviceIdType.MESH
F32, BF16 = jnp.float32, jnp.bfloat16

D_IN, D_OUT, RANK, REPLICAS = 8192, 6144, 32, 8
TOK, FEAT, OWN = 1024, 512, 64
CW = 512
NC = D_OUT // CW
NT = (((1,), (1,)), ((), ()))

STAGE_AT = dict(a=1, b=2, c=3, d=4, e=5, f=6, g=7, h=8, i=9, j=10)


def place():
    d, t = lax.axis_index("dp"), lax.axis_index("tensor")
    return dict(y_lo=d // 4, z=d % 4, x=t // 4, y_hi=(t // 2) % 2, core=t % 2)


def device(at, **moved):
    q = {**at, **moved}
    return {"dp": q["y_lo"] * 4 + q["z"], "tensor": q["x"] * 4 + q["y_hi"] * 2 + q["core"]}


def along_y(at, by):
    y = (at["y_hi"] * 2 + at["y_lo"] + by) % 4
    return device(at, y_hi=y // 2, y_lo=y % 2)


def split3(v):
    hi = v.astype(BF16)
    rest = v - hi.astype(F32)
    mid = rest.astype(BF16)
    low = (rest - mid.astype(F32)).astype(BF16)
    return hi, mid, low


def rows3(v):
    return jnp.concatenate(split3(v), axis=0)


def sum3(v):
    n = v.shape[0] // 3
    return v[:n] + (v[n : 2 * n] + v[2 * n :])


def dot(a, b, dims=(((1,), (0,)), ((), ()))):
    return lax.dot_general(a, b, dims, preferred_element_type=F32)


def kernel(
    acts_hbm, grad_hbm, weight_hbm, residue_hbm, qt_hbm,
    gin_hbm, pt_ref, qt_out_ref, new_hbm,
    g, weight, residue, merged, acts, acts_t, gin, gin_out, stage,
    qt, qt3, gq, gq3, part, sk_z, sk_y, st, st3, z_out, z_in, gram_in, gram_core, linv,
    b_own, b_core, b_z, piece_z, b_y, piece_y, b_x, q_all, b_t, q6, p6,
    load_sem, bulk_send, bulk_recv, core_send, core_recv, own_sem,
    gq_send, gq_recv, z_send, z_recv, gr_send, gr_recv, ring_send, ring_recv, pair_send, pair_recv, out_sem,
):
    at = place()
    x, y_hi, y_lo, z, core = at["x"], at["y_hi"], at["y_lo"], at["z"], at["core"]
    y = y_hi * 2 + y_lo
    me = x * 4 + y_hi * 2 + core
    chip = x * 2 + y_hi
    other = device(at, core=1 - core)
    peers = [(dx, dy) for dx in range(4) for dy in range(2) if (dx, dy) != (0, 0)]
    peer_ids = [device(at, x=(x + dx) % 4, y_hi=(y_hi + dy) % 2) for dx, dy in peers]
    ring = {
        "x": [device(at, x=(x + i) % 4) for i in (1, 2, 3)],
        "y": [along_y(at, i) for i in (1, 2, 3)],
        "z": [device(at, z=(z + i) % 4) for i in (1, 2, 3)],
    }

    def own_rows(dx, dy):
        t = ((x + dx + 4) % 4) * 4 + ((y_hi + dy) % 2) * 2 + core
        return pl.ds(pl.multiple_of(t * OWN, OWN), OWN)

    mine = own_rows(0, 0)
    chip_rows = pl.ds(pl.multiple_of(chip * 2 * OWN, 2 * OWN), 2 * OWN)

    def chunk(k):
        return pl.ds(pl.multiple_of(k * CW, CW), CW)

    for k in range(NC):
        pltpu.make_async_copy(
            grad_hbm.at[:, pl.ds(k * CW, CW)], g.at[k, mine], load_sem.at[0]
        ).start()
    load_q = pltpu.make_async_copy(qt_hbm, qt, load_sem.at[1])
    load_res = pltpu.make_async_copy(residue_hbm, residue, load_sem.at[2])
    load_acts = pltpu.make_async_copy(acts_hbm, acts, load_sem.at[3])
    load_w = pltpu.make_async_copy(weight_hbm, weight, load_sem.at[4])
    load_q.start()
    load_acts.start()
    load_res.start()
    load_w.start()

    barrier = pltpu.get_barrier_semaphore()
    greet = [*peer_ids, other, ring["y"][0], ring["y"][2], *ring["z"]]
    for who in greet:
        pl.semaphore_signal(barrier, inc=1, device_id=who, device_id_type=MESH)
    pl.semaphore_wait(barrier, len(greet))

    def remote(src, dst, send, recv, who):
        return pltpu.make_async_remote_copy(
            src_ref=src, dst_ref=dst, send_sem=send, recv_sem=recv, device_id=who, device_id_type=MESH
        )

    def bulk(flow, k, rows, who):
        block = g.at[k, rows]
        return remote(block, block, bulk_send.at[flow], bulk_recv.at[flow, k], who)

    def arrived(flow, k):
        bulk(flow, k, mine, other).wait_recv()

    def to_core(k, rows):
        block = g.at[k, rows]
        remote(block, block, core_send.at[0], core_recv.at[k], other).start()

    right, left, across = ring["x"][0], ring["x"][2], device(at, y_hi=1 - y_hi)

    pltpu.make_async_copy(g.at[:, mine], g.at[:, mine], load_sem.at[0]).wait()
    own_copy = remote(g.at[:, mine], g.at[:, mine], own_sem.at[0], own_sem.at[1], other)
    own_copy.start()
    load_q.wait()
    qt3[...] = rows3(qt[...])

    def step(s, carry):
        @pl.when(s < NC)
        def _():
            bulk(0, s, mine, right).start()
            bulk(1, s, mine, left).start()
            bulk(2, s, mine, across).start()

        @pl.when(s == 0)
        def _():
            own_copy.wait_recv()
            total = jnp.zeros((3 * RANK, 2 * OWN), F32)
            for k in range(NC):
                total += dot(qt3[:, k * CW : (k + 1) * CW], g[k, chip_rows, :], NT)
            gq[chip] = sum3(total)
            for i, who in enumerate(peer_ids):
                remote(gq.at[chip], gq.at[chip], gq_send.at[i], gq_recv.at[i], who).start()
            load_res.wait()

            def add(k, total):
                return total + dot(qt3[:, chunk(k)], residue[:, chunk(k)], NT)

            part[...] = sum3(lax.fori_loop(0, NC, add, jnp.zeros((3 * RANK, FEAT), F32)))
            load_acts.wait()
            acts_t[...] = acts[...].T
            gin[...] = jnp.zeros_like(gin)

        @pl.when((s >= 1) & (s <= NC))
        def _():
            k = s - 1
            arrived(0, k)
            arrived(1, k)
            odd = k % 2
            ahead = device(at, x=(x + 1 + 2 * odd) % 4)
            bulk(3, k, own_rows(2 * odd - 1, 0), ahead).start()
            arrived(2, k)
            bulk(4, k, own_rows(0, 1), right).start()
            bulk(5, k, own_rows(0, 1), left).start()
            to_core(k, own_rows(-1, 0))
            to_core(k, own_rows(1, 0))
            to_core(k, own_rows(0, 1))

        @pl.when((s >= 2) & (s <= NC + 1))
        def _():
            k = s - 2
            arrived(3, k)
            bulk(6, k, own_rows(2, 0), across).start()
            to_core(k, own_rows(2, 0))
            arrived(4, k)
            to_core(k, own_rows(-1, 1))
            arrived(5, k)
            to_core(k, own_rows(1, 1))

        @pl.when((s >= 3) & (s <= NC + 2))
        def _():
            k = s - 3
            arrived(6, k)
            to_core(k, own_rows(2, 1))

        @pl.when(s == 4)
        def _():
            load_w.wait()

        @pl.when(s >= 4)
        def _():
            k = s - 4
            landed = g.at[k, pl.ds(0, 7 * OWN)]
            remote(landed, landed, core_send.at[0], core_recv.at[k], other).wait_recv()
            merged[k] = dot(acts_t[...], g[k]) + residue[:, chunk(k)].astype(F32)
            gin[...] += dot(g[k], weight[:, chunk(k)], NT)

        def stage_at(name):
            return pl.when(s == STAGE_AT[name])

        @stage_at("a")
        def _():
            for i, who in enumerate(peer_ids):
                remote(gq.at[chip], gq.at[chip], gq_send.at[i], gq_recv.at[i], who).wait()
            for j in range(8):
                gq3[:, j * 128 : (j + 1) * 128] = rows3(gq[j])
            sk_z[z] = part[...] + sum3(dot(gq3[...], acts[...]))
            for i, who in enumerate(ring["z"]):
                remote(sk_z.at[z], sk_z.at[z], ring_send.at[0, i], ring_recv.at[0, i], who).start()

        @stage_at("b")
        def _():
            for i, who in enumerate(ring["z"]):
                remote(sk_z.at[z], sk_z.at[z], ring_send.at[0, i], ring_recv.at[0, i], who).wait()
            sk_y[y_lo] = (sk_z[0] + sk_z[1]) + (sk_z[2] + sk_z[3])
            remote(sk_y.at[y_lo], sk_y.at[y_lo], pair_send.at[0], pair_recv.at[0], device(at, y_lo=1 - y_lo)).start()

        @stage_at("c")
        def _():
            remote(sk_y.at[y_lo], sk_y.at[y_lo], pair_send.at[0], pair_recv.at[0], device(at, y_lo=1 - y_lo)).wait()
            sketch = (sk_y[0] + sk_y[1]) * (1.0 / REPLICAS)
            st[...] = sketch
            st3[...] = rows3(sketch)
            zt = sum3(dot(st3[...], acts_t[...]))
            for j in range(8):
                z_out[j] = zt[:, j * 128 : (j + 1) * 128]
            for i, who in enumerate(peer_ids):
                dx, dy = peers[i]
                there = ((x + dx) % 4) * 2 + (y_hi + dy) % 2
                remote(z_out.at[there], z_in.at[chip], z_send.at[i], z_recv.at[i], who).start()
            z_in[chip] = z_out[chip]
            gram_in[chip] = jnp.zeros((RANK, 128), F32)
            gram_in[chip, :, 0:RANK] = lax.dot_general(
                sketch, sketch, NT, precision=lax.Precision.HIGHEST, preferred_element_type=F32
            )
            for i, who in enumerate(peer_ids):
                remote(gram_in.at[chip], gram_in.at[chip], gr_send.at[i], gr_recv.at[i], who).start()

            def from_residue(k, _):
                r = sum3(dot(st3[...], residue[:, chunk(k)]))
                for i in range(CW // 128):
                    b_own[2 * (k * 4 + i)] = r[0:16, i * 128 : (i + 1) * 128]
                    b_own[2 * (k * 4 + i) + 1] = r[16:32, i * 128 : (i + 1) * 128]
                return 0

            lax.fori_loop(0, NC, from_residue, 0)

        half = pl.ds(core * 48, 48)
        half_there = pl.ds((1 - core) * 48, 48)

        @stage_at("d")
        def _():
            for i, who in enumerate(peer_ids):
                remote(z_out.at[0], z_in.at[0], z_send.at[i], z_recv.at[i], who).wait()
            total = z_in[0]
            for j in range(1, 8):
                total = total + z_in[j]
            z3 = rows3(total)

            def from_grad(k, _):
                r = sum3(dot(z3, g[k, chip_rows, :]))
                for i in range(CW // 128):
                    b_own[2 * (k * 4 + i)] += r[0:16, i * 128 : (i + 1) * 128]
                    b_own[2 * (k * 4 + i) + 1] += r[16:32, i * 128 : (i + 1) * 128]
                return 0

            lax.fori_loop(0, NC, from_grad, 0)
            remote(b_own.at[half_there], b_core, pair_send.at[1], pair_recv.at[1], other).start()
            for i, who in enumerate(peer_ids):
                remote(gram_in.at[chip], gram_in.at[chip], gr_send.at[i], gr_recv.at[i], who).wait()
            total = gram_in[0]
            for j in range(1, 8):
                total = total + gram_in[j]
            gram_core[core] = total
            remote(gram_core.at[core], gram_core.at[core], pair_send.at[2], pair_recv.at[2], other).start()

        @stage_at("e")
        def _():
            remote(b_own.at[half_there], b_core, pair_send.at[1], pair_recv.at[1], other).wait()
            b_core[...] += b_own[half]
            for i, who in enumerate(ring["z"]):
                there = pl.ds(((z + i + 1) % 4) * 12, 12)
                remote(b_core.at[there], b_z.at[i], ring_send.at[1, i], ring_recv.at[1, i], who).start()
            remote(gram_core.at[core], gram_core.at[core], pair_send.at[2], pair_recv.at[2], other).wait()
            gram = (gram_core[0] + gram_core[1]) * (1.0 / D_IN)
            sub = lax.broadcasted_iota(jnp.int32, (RANK, 128), 0)
            lane = lax.broadcasted_iota(jnp.int32, (RANK, 128), 1)
            unit = jnp.where(sub == lane, 1.0, 0.0).astype(F32)

            def eliminate(j, both):
                a, e = both
                row_a = jnp.sum(jnp.where(sub == j, a, 0.0), axis=0, keepdims=True)
                row_e = jnp.sum(jnp.where(sub == j, e, 0.0), axis=0, keepdims=True)
                col = jnp.sum(jnp.where(lane == j, a, 0.0), axis=1, keepdims=True)
                diag = jnp.sum(jnp.where(lane[0:1] == j, row_a, 0.0), axis=1, keepdims=True)
                scale = 1.0 / jnp.sqrt(diag)
                row_a, row_e = row_a * scale, row_e * scale
                factor = jnp.where(sub > j, col * scale, 0.0)
                a = jnp.where(sub == j, row_a, a - factor * row_a)
                e = jnp.where(sub == j, row_e, e - factor * row_e)
                return a, e

            linv[...] = lax.fori_loop(0, RANK, eliminate, (gram, unit))[1]

        @stage_at("f")
        def _():
            for i, who in enumerate(ring["z"]):
                remote(b_z.at[i], b_z.at[i], ring_send.at[1, i], ring_recv.at[1, i], who).wait()
            piece_z[...] = (b_core[pl.ds(z * 12, 12)] + b_z[0]) + (b_z[1] + b_z[2])
            for i, who in enumerate(ring["y"]):
                there = pl.ds(((y + i + 1) % 4) * 3, 3)
                remote(piece_z.at[there], b_y.at[i], ring_send.at[2, i], ring_recv.at[2, i], who).start()

        @stage_at("g")
        def _():
            for i, who in enumerate(ring["y"]):
                remote(b_y.at[i], b_y.at[i], ring_send.at[2, i], ring_recv.at[2, i], who).wait()
            b_x[x] = (piece_z[pl.ds(y * 3, 3)] + b_y[0]) + (b_y[1] + b_y[2])
            for i, who in enumerate(ring["x"]):
                remote(b_x.at[x], b_x.at[x], ring_send.at[3, i], ring_recv.at[3, i], who).start()

        piece = pl.ds(core * 48 + z * 12 + y * 3, 3)
        pieces = pl.ds(core * 48 + z * 12, 12)

        @stage_at("h")
        def _():
            for i, who in enumerate(ring["x"]):
                remote(b_x.at[x], b_x.at[x], ring_send.at[3, i], ring_recv.at[3, i], who).wait()
            q_all[piece] = (b_x[0] + b_x[1]) + (b_x[2] + b_x[3])
            for i, who in enumerate(ring["y"]):
                remote(q_all.at[piece], q_all.at[piece], ring_send.at[4, i], ring_recv.at[4, i], who).start()

        @stage_at("i")
        def _():
            for i, who in enumerate(ring["y"]):
                remote(q_all.at[piece], q_all.at[piece], ring_send.at[4, i], ring_recv.at[4, i], who).wait()
            for i, who in enumerate(ring["z"]):
                remote(q_all.at[pieces], q_all.at[pieces], ring_send.at[5, i], ring_recv.at[5, i], who).start()

        @stage_at("j")
        def _():
            for i, who in enumerate(ring["z"]):
                remote(q_all.at[pieces], q_all.at[pieces], ring_send.at[5, i], ring_recv.at[5, i], who).wait()
            remote(q_all.at[half], q_all.at[half], pair_send.at[3], pair_recv.at[3], other).start()

        return carry

    lax.fori_loop(0, NC + 4, step, 0)

    gin_out[...] = gin[...].astype(BF16)
    store_gin = pltpu.make_async_copy(gin_out, gin_hbm, out_sem.at[2])
    store_gin.start()

    inverse = linv[:, 0:RANK]
    ih, im, il = split3(inverse)
    i6 = jnp.concatenate([ih, ih, im, ih, il, im], axis=1)

    def stack6(v):
        h, m, low = split3(v)
        return jnp.concatenate([h, m, h, low, h, m], axis=0)

    p_t = dot(i6, stack6(st[...]))
    pt_ref[...] = p_t
    ph, pm, pw = split3(p_t)
    p6[...] = jnp.concatenate([ph, ph, pm, ph, pw, pm], axis=0).T

    half = pl.ds(core * 48, 48)
    remote(q_all.at[half], q_all.at[half], pair_send.at[3], pair_recv.at[3], other).wait()

    def store(k, slot):
        return pltpu.make_async_copy(stage.at[slot], new_hbm.at[:, chunk(k)], out_sem.at[slot])

    def finish(k, carry):
        for i in range(CW // 128):
            b_t[0:16, i * 128 : (i + 1) * 128] = q_all[2 * (k * 4 + i)]
            b_t[16:32, i * 128 : (i + 1) * 128] = q_all[2 * (k * 4 + i) + 1]
        q_t = dot(i6, stack6(b_t[...])) * (1.0 / (REPLICAS * math.sqrt(D_IN)))
        qt_out_ref[:, chunk(k)] = q_t
        q6[...] = stack6(q_t * (1.0 / math.sqrt(D_IN)))
        slot = k % 2

        @pl.when(k >= 2)
        def _():
            store(k - 2, slot).wait()

        stage[slot] = (merged[k] - dot(p6[...], q6[...])).astype(BF16)
        store(k, slot).start()
        return carry

    lax.fori_loop(0, NC, finish, 0)
    store(NC - 2, 0).wait()
    store(NC - 1, 1).wait()
    store_gin.wait()

    own_copy.wait_send()
    for flow in range(7):
        block = g.at[:, pl.ds(0, OWN)]
        remote(block, block, bulk_send.at[flow], bulk_recv.at[flow, 0], other).wait_send()
    block = g.at[:, pl.ds(0, 7 * OWN)]
    remote(block, block, core_send.at[0], core_recv.at[0], other).wait_send()


def shards(acts, grad_out, weight, residue, start_q):
    vmem, dma = pltpu.VMEM, pltpu.SemaphoreType.DMA
    hbm = pl.BlockSpec(memory_space=pl.ANY)
    here = pl.BlockSpec(memory_space=pltpu.VMEM)
    flops = 4 * TOK * FEAT * D_OUT
    grad_in, p_t, q_t, new = pl.pallas_call(
        kernel,
        out_shape=[
            jax.ShapeDtypeStruct((TOK, FEAT), BF16),
            jax.ShapeDtypeStruct((RANK, FEAT), F32),
            jax.ShapeDtypeStruct((RANK, D_OUT), F32),
            jax.ShapeDtypeStruct((FEAT, D_OUT), BF16),
        ],
        in_specs=[hbm] * 5,
        out_specs=[hbm, here, here, hbm],
        scratch_shapes=[
            vmem((NC, TOK, CW), BF16),
            vmem((FEAT, D_OUT), BF16),
            vmem((FEAT, D_OUT), BF16),
            vmem((NC, FEAT, CW), F32),
            vmem((TOK, FEAT), BF16),
            vmem((FEAT, TOK), BF16),
            vmem((TOK, FEAT), F32),
            vmem((TOK, FEAT), BF16),
            vmem((2, FEAT, CW), BF16),
            vmem((RANK, D_OUT), F32),
            vmem((3 * RANK, D_OUT), BF16),
            vmem((8, RANK, 128), F32),
            vmem((3 * RANK, TOK), BF16),
            vmem((RANK, FEAT), F32),
            vmem((4, RANK, FEAT), F32),
            vmem((2, RANK, FEAT), F32),
            vmem((RANK, FEAT), F32),
            vmem((3 * RANK, FEAT), BF16),
            vmem((8, RANK, 128), F32),
            vmem((8, RANK, 128), F32),
            vmem((8, RANK, 128), F32),
            vmem((2, RANK, 128), F32),
            vmem((RANK, 128), F32),
            vmem((96, 16, 128), F32),
            vmem((48, 16, 128), F32),
            vmem((3, 12, 16, 128), F32),
            vmem((12, 16, 128), F32),
            vmem((3, 3, 16, 128), F32),
            vmem((3, 16, 128), F32),
            vmem((4, 3, 16, 128), F32),
            vmem((96, 16, 128), F32),
            vmem((RANK, CW), F32),
            vmem((6 * RANK, CW), BF16),
            vmem((FEAT, 6 * RANK), BF16),
            dma((5,)),
            dma((7,)),
            dma((7, NC)),
            dma((1,)),
            dma((NC,)),
            dma((2,)),
            dma((7,)),
            dma((7,)),
            dma((7,)),
            dma((7,)),
            dma((7,)),
            dma((7,)),
            dma((6, 3)),
            dma((6, 3)),
            dma((4,)),
            dma((4,)),
            dma((3,)),
        ],
        compiler_params=pltpu.CompilerParams(
            collective_id=1, has_side_effects=True, vmem_limit_bytes=60 * 2**20
        ),
        cost_estimate=pl.CostEstimate(flops=flops, bytes_accessed=24 * 2**20, transcendentals=0),
        name="gather_and_compress",
    )(acts, grad_out, weight, residue[0], start_q.T)
    return grad_in, p_t.T, q_t.T, new[None]


def solution(mesh):
    in_specs = (
        P("dp", "tensor"),
        P(("dp", "tensor"), None),
        P("tensor", None),
        P("dp", "tensor", None),
        P(),
    )
    out_specs = (P("dp", "tensor"), P("tensor", None), P(), P("dp", "tensor", None))
    return jax.shard_map(shards, mesh=mesh, in_specs=in_specs, out_specs=out_specs, check_vma=False)
```

```python
import math

import jax
import jax.numpy as jnp
from jax import lax
from jax.experimental import pallas as pl
from jax.experimental.pallas import tpu as pltpu
from jax.sharding import PartitionSpec as P

MESH = pl.DeviceIdType.MESH
F32, BF16 = jnp.float32, jnp.bfloat16

D_IN, D_OUT, RANK, REPLICAS = 8192, 6144, 32, 8
TOK, FEAT, OWN = 1024, 512, 64
CW = 512
NC = D_OUT // CW
NT = (((1,), (1,)), ((), ()))

STAGE_AT = dict(a=1, b=3, c=4, d=5, e=8, f=7, g=8, h=9, i=10, j=11, k=12)
PARTS = 3
TILES = D_OUT // 128 * RANK // 8
PART = TILES // 2 // PARTS
STEPS = NC + 7
EARLY = 3
FINISH_FROM, FINISH_EACH = 13, 2
DONE = (STEPS - FINISH_FROM) * FINISH_EACH


def place():
    d, t = lax.axis_index("dp"), lax.axis_index("tensor")
    return dict(y_lo=d // 4, z=d % 4, x=t // 4, y_hi=(t // 2) % 2, core=t % 2)


def device(at, **moved):
    q = {**at, **moved}
    return {"dp": q["y_lo"] * 4 + q["z"], "tensor": q["x"] * 4 + q["y_hi"] * 2 + q["core"]}


def along_y(at, by):
    y = (at["y_hi"] * 2 + at["y_lo"] + by) % 4
    return device(at, y_hi=y // 2, y_lo=y % 2)


def split3(v):
    hi = v.astype(BF16)
    rest = v - hi.astype(F32)
    mid = rest.astype(BF16)
    low = (rest - mid.astype(F32)).astype(BF16)
    return hi, mid, low


def rows3(v):
    return jnp.concatenate(split3(v), axis=0)


def sum3(v):
    n = v.shape[0] // 3
    return v[:n] + (v[n : 2 * n] + v[2 * n :])


def dot(a, b, dims=(((1,), (0,)), ((), ()))):
    return lax.dot_general(a, b, dims, preferred_element_type=F32)


def kernel(
    acts_hbm, grad_hbm, weight_hbm, residue_hbm, qt_hbm,
    gin_out, pt_ref, qt_out_ref, new_ref,
    g, weight, merged, acts_t, gin,
    qt3, gq, gq3, part, sk_z, sk_y, st, st3, z_out, z_in, gram_in, gram_core, gram_all, linv, i6,
    b_own, b_core, b_z, piece_z, b_y, b_x, q_all, b_t, q6, p6,
    load_sem, bulk_send, bulk_recv, core_send, core_recv, own_sem,
    gq_send, gq_recv, z_send, z_recv, gr_send, gr_recv, ring_send, ring_recv, pair_send, pair_recv,
    bc_send, bc_recv, rs_send, rs_recv, qc_send, qc_recv,
):
    acts, qt, residue = gin_out, qt_out_ref, new_ref
    at = place()
    x, y_hi, y_lo, z, core = at["x"], at["y_hi"], at["y_lo"], at["z"], at["core"]
    y = y_hi * 2 + y_lo
    me = x * 4 + y_hi * 2 + core
    chip = x * 2 + y_hi
    other = device(at, core=1 - core)
    peers = [(dx, dy) for dx in range(4) for dy in range(2) if (dx, dy) != (0, 0)]
    peer_ids = [device(at, x=(x + dx) % 4, y_hi=(y_hi + dy) % 2) for dx, dy in peers]
    ring = {
        "x": [device(at, x=(x + i) % 4) for i in (1, 2, 3)],
        "y": [along_y(at, i) for i in (1, 2, 3)],
        "z": [device(at, z=(z + i) % 4) for i in (1, 2, 3)],
    }

    def own_rows(dx, dy):
        t = ((x + dx + 4) % 4) * 4 + ((y_hi + dy) % 2) * 2 + core
        return pl.ds(pl.multiple_of(t * OWN, OWN), OWN)

    mine = own_rows(0, 0)
    chip_rows = pl.ds(pl.multiple_of(chip * 2 * OWN, 2 * OWN), 2 * OWN)

    def chunk(k):
        return pl.ds(pl.multiple_of(k * CW, CW), CW)

    for k in range(NC):
        pltpu.make_async_copy(
            grad_hbm.at[:, pl.ds(k * CW, CW)], g.at[k, mine], load_sem.at[0]
        ).start()
    load_q = pltpu.make_async_copy(qt_hbm, qt, load_sem.at[1])
    load_res = pltpu.make_async_copy(residue_hbm, residue, load_sem.at[2])
    load_acts = pltpu.make_async_copy(acts_hbm, acts, load_sem.at[3])
    load_w = pltpu.make_async_copy(weight_hbm, weight, load_sem.at[4])
    load_q.start()
    load_acts.start()
    load_res.start()
    load_w.start()

    barrier = pltpu.get_barrier_semaphore()
    greet = [*peer_ids, other, ring["y"][0], ring["y"][2], *ring["z"]]
    for who in greet:
        pl.semaphore_signal(barrier, inc=1, device_id=who, device_id_type=MESH)
    load_q.wait()
    qt3[...] = rows3(qt[...])
    pltpu.make_async_copy(g.at[:, mine], g.at[:, mine], load_sem.at[0]).wait()
    pl.semaphore_wait(barrier, len(greet))

    def remote(src, dst, send, recv, who):
        return pltpu.make_async_remote_copy(
            src_ref=src, dst_ref=dst, send_sem=send, recv_sem=recv, device_id=who, device_id_type=MESH
        )

    def bulk(flow, k, rows, who):
        block = g.at[k, rows]
        return remote(block, block, bulk_send.at[flow], bulk_recv.at[flow, k], who)

    def arrived(flow, k):
        bulk(flow, k, mine, other).wait_recv()

    def to_core(k, rows):
        block = g.at[k, rows]
        remote(block, block, core_send.at[0], core_recv.at[k], other).start()

    right, left, across = ring["x"][0], ring["x"][2], device(at, y_hi=1 - y_hi)

    own_copy = remote(g.at[:, mine], g.at[:, mine], own_sem.at[0], own_sem.at[1], other)
    own_copy.start()

    def stack6(v):
        h, m, low = split3(v)
        return jnp.concatenate([h, m, h, low, h, m], axis=0)

    def finish(k):
        for i in range(CW // 128):
            block = q_all[pl.ds(k * (CW // 32) + 4 * i, 4)]
            b_t[:, i * 128 : (i + 1) * 128] = block.reshape(RANK, 128)
        q_t = dot(i6[...], stack6(b_t[...])) * (1.0 / (REPLICAS * math.sqrt(D_IN)))
        qt_out_ref[:, chunk(k)] = q_t
        q6[...] = stack6(q_t * (1.0 / math.sqrt(D_IN)))
        new_ref[:, chunk(k)] = (merged[k] - dot(p6[...], q6[...])).astype(BF16)

    def send_own(k):
        bulk(0, k, mine, right).start()
        bulk(1, k, mine, left).start()
        bulk(2, k, mine, across).start()

    def step(s, carry):
        @pl.when((s >= EARLY) & (s < NC))
        def _():
            send_own(s)

        @pl.when(s == 0)
        def _():
            send_own(0)
            own_copy.wait_recv()
            total = jnp.zeros((3 * RANK, 2 * OWN), F32)
            for k in range(NC):
                total += dot(qt3[:, k * CW : (k + 1) * CW], g[k, chip_rows, :], NT)
            gq[chip] = sum3(total)
            for i, who in enumerate(peer_ids):
                remote(gq.at[chip], gq.at[chip], gq_send.at[i], gq_recv.at[i], who).start()
            for k in range(1, EARLY):
                send_own(k)
            load_res.wait()

            def add(k, total):
                return total + dot(qt3[:, chunk(k)], residue[:, chunk(k)], NT)

            part[...] = sum3(lax.fori_loop(0, NC, add, jnp.zeros((3 * RANK, FEAT), F32)))
            load_acts.wait()
            acts_t[...] = acts[...].T
            gin[...] = jnp.zeros_like(gin)

        @pl.when((s >= 2) & (s < NC + 2))
        def _():
            k = s - 2
            arrived(0, k)
            arrived(1, k)
            odd = k % 2
            ahead = device(at, x=(x + 1 + 2 * odd) % 4)
            bulk(3, k, own_rows(2 * odd - 1, 0), ahead).start()
            arrived(2, k)
            bulk(4, k, own_rows(0, 1), right).start()
            bulk(5, k, own_rows(0, 1), left).start()
            to_core(k, own_rows(-1, 0))
            to_core(k, own_rows(1, 0))
            to_core(k, own_rows(0, 1))

        @pl.when((s >= 4) & (s < NC + 4))
        def _():
            k = s - 4
            arrived(3, k)
            bulk(6, k, own_rows(2, 0), across).start()
            to_core(k, own_rows(2, 0))
            arrived(4, k)
            to_core(k, own_rows(-1, 1))
            arrived(5, k)
            to_core(k, own_rows(1, 1))

        @pl.when((s >= 6) & (s < NC + 6))
        def _():
            k = s - 6
            arrived(6, k)
            to_core(k, own_rows(2, 1))

        @pl.when(s == 4)
        def _():
            load_w.wait()

        @pl.when(s >= 7)
        def _():
            k = s - 7
            landed = g.at[k, pl.ds(0, 7 * OWN)]
            remote(landed, landed, core_send.at[0], core_recv.at[k], other).wait_recv()
            merged[k] = dot(acts_t[...], g[k]) + residue[:, chunk(k)].astype(F32)
            gin[...] += dot(g[k], weight[:, chunk(k)], NT)

        def stage_at(name):
            return pl.when(s == STAGE_AT[name])

        @stage_at("a")
        def _():
            for i, who in enumerate(peer_ids):
                remote(gq.at[chip], gq.at[chip], gq_send.at[i], gq_recv.at[i], who).wait()
            for j in range(8):
                gq3[:, j * 128 : (j + 1) * 128] = rows3(gq[j])
            sk_z[z] = part[...] + sum3(dot(gq3[...], acts[...]))
            for i, who in enumerate(ring["z"]):
                remote(sk_z.at[z], sk_z.at[z], ring_send.at[0, i], ring_recv.at[0, i], who).start()

        @stage_at("b")
        def _():
            for i, who in enumerate(ring["z"]):
                remote(sk_z.at[z], sk_z.at[z], ring_send.at[0, i], ring_recv.at[0, i], who).wait()
            sk_y[y_lo] = (sk_z[0] + sk_z[1]) + (sk_z[2] + sk_z[3])
            remote(sk_y.at[y_lo], sk_y.at[y_lo], pair_send.at[0], pair_recv.at[0], device(at, y_lo=1 - y_lo)).start()

        @stage_at("c")
        def _():
            remote(sk_y.at[y_lo], sk_y.at[y_lo], pair_send.at[0], pair_recv.at[0], device(at, y_lo=1 - y_lo)).wait()
            sketch = (sk_y[0] + sk_y[1]) * (1.0 / REPLICAS)
            st[...] = sketch
            st3[...] = rows3(sketch)
            zt = sum3(dot(st3[...], acts_t[...]))
            for j in range(8):
                z_out[j] = zt[:, j * 128 : (j + 1) * 128]
            for i, who in enumerate(peer_ids):
                dx, dy = peers[i]
                there = ((x + dx) % 4) * 2 + (y_hi + dy) % 2
                remote(z_out.at[there], z_in.at[chip], z_send.at[i], z_recv.at[i], who).start()
            z_in[chip] = z_out[chip]
            gram = lax.dot_general(
                sketch, sketch, NT, precision=lax.Precision.HIGHEST, preferred_element_type=F32
            )
            for i in range(4):
                gram_in[chip, :, i * RANK : (i + 1) * RANK] = gram[i * 8 : (i + 1) * 8]
            for i, who in enumerate(peer_ids):
                remote(gram_in.at[chip], gram_in.at[chip], gr_send.at[i], gr_recv.at[i], who).start()

            def from_residue(k, _):
                r = sum3(dot(st3[...], residue[:, chunk(k)]))
                for i in range(CW // 128):
                    b_own[pl.ds(k * (CW // 32) + 4 * i, 4)] = r[:, i * 128 : (i + 1) * 128].reshape(4, 8, 128)
                return 0

            lax.fori_loop(0, NC, from_residue, 0)

        def tiles(c, h):
            return pl.ds(c * (TILES // 2) + h * PART, PART)

        def fourth(i):
            return pl.ds(i * (PART // 4), PART // 4)

        def core_copy(h, start):
            c = remote(b_own.at[tiles(1 - core, h)], b_core.at[h], bc_send.at[h], bc_recv.at[h], other)
            c.start() if start else c.wait()

        @stage_at("d")
        def _():
            for i, who in enumerate(peer_ids):
                remote(z_out.at[0], z_in.at[0], z_send.at[i], z_recv.at[i], who).wait()
            total = z_in[0]
            for j in range(1, 8):
                total = total + z_in[j]
            z3 = rows3(total)

            def from_grad(k, _):
                r = sum3(dot(z3, g[k, chip_rows, :]))
                for i in range(CW // 128):
                    b_own[pl.ds(k * (CW // 32) + 4 * i, 4)] += r[:, i * 128 : (i + 1) * 128].reshape(4, 8, 128)
                return 0

            each = NC // 2 // PARTS
            first = (1 - core) * (NC // 2)
            for h in range(PARTS):
                lax.fori_loop(first + h * each, first + (h + 1) * each, from_grad, 0)
                core_copy(h, True)
            lax.fori_loop(core * (NC // 2), (core + 1) * (NC // 2), from_grad, 0)
            for i, who in enumerate(peer_ids):
                remote(gram_in.at[chip], gram_in.at[chip], gr_send.at[i], gr_recv.at[i], who).wait()
            total = gram_in[0]
            for j in range(1, 8):
                total = total + gram_in[j]
            gram_core[core] = total
            remote(gram_core.at[core], gram_core.at[core], pair_send.at[2], pair_recv.at[2], other).start()

            for h in range(PARTS):
                core_copy(h, False)
                b_core[h] += b_own[tiles(core, h)]
                for i, who in enumerate(ring["z"]):
                    there = fourth((z + i + 1) % 4)
                    remote(b_core.at[h, there], b_z.at[h, i], rs_send.at[0, h, i], rs_recv.at[0, h, i], who).start()
        @stage_at("e")
        def _():
            remote(gram_core.at[core], gram_core.at[core], pair_send.at[2], pair_recv.at[2], other).wait()
            packed = (gram_core[0] + gram_core[1]) * (1.0 / D_IN)
            gram_all[...] = jnp.zeros((RANK, 128), F32)
            for i in range(4):
                gram_all[i * 8 : (i + 1) * 8, 0:RANK] = packed[:, i * RANK : (i + 1) * RANK]
            sub = lax.broadcasted_iota(jnp.int32, (RANK, 128), 0)
            lane = lax.broadcasted_iota(jnp.int32, (RANK, 128), 1)
            unit = jnp.where(sub == lane, 1.0, 0.0).astype(F32)

            def eliminate(j, both):
                a, e = both
                row_a = jnp.sum(jnp.where(sub == j, a, 0.0), axis=0, keepdims=True)
                row_e = jnp.sum(jnp.where(sub == j, e, 0.0), axis=0, keepdims=True)
                col = jnp.sum(jnp.where(lane == j, a, 0.0), axis=1, keepdims=True)
                diag = jnp.sum(jnp.where(lane[0:1] == j, row_a, 0.0), axis=1, keepdims=True)
                scale = 1.0 / jnp.sqrt(diag)
                row_a, row_e = row_a * scale, row_e * scale
                factor = jnp.where(sub > j, col * scale, 0.0)
                a = jnp.where(sub == j, row_a, a - factor * row_a)
                e = jnp.where(sub == j, row_e, e - factor * row_e)
                return a, e

            linv[...] = lax.fori_loop(0, RANK, eliminate, (gram_all[...], unit))[1]
            ih, im, il = split3(linv[:, 0:RANK])
            i6[...] = jnp.concatenate([ih, ih, im, ih, il, im], axis=1)
            p_t = dot(i6[...], stack6(st[...]))
            pt_ref[...] = p_t
            ph, pm, pw = split3(p_t)
            p6[...] = jnp.concatenate([ph, ph, pm, ph, pw, pm], axis=0).T

        def landed_at(axis, stage, h, ref):
            for i, who in enumerate(ring[axis]):
                remote(ref(i), ref(i), rs_send.at[stage, h, i], rs_recv.at[stage, h, i], who).wait()

        @stage_at("f")
        def _():
            for h in range(PARTS):
                landed_at("z", 0, h, lambda i: b_z.at[h, i])
                piece_z[h] = (b_core[h, fourth(z)] + b_z[h, 0]) + (b_z[h, 1] + b_z[h, 2])
                for i, who in enumerate(ring["y"]):
                    there = pl.ds(((y + i + 1) % 4) * (PART // 16), PART // 16)
                    remote(piece_z.at[h, there], b_y.at[h, i], rs_send.at[1, h, i], rs_recv.at[1, h, i], who).start()

        @stage_at("g")
        def _():
            for h in range(PARTS):
                landed_at("y", 1, h, lambda i: b_y.at[h, i])
                own = piece_z[h, pl.ds(y * (PART // 16), PART // 16)]
                b_x[h, x] = (own + b_y[h, 0]) + (b_y[h, 1] + b_y[h, 2])
                for i, who in enumerate(ring["x"]):
                    block = b_x.at[h, x]
                    remote(block, block, rs_send.at[2, h, i], rs_recv.at[2, h, i], who).start()

        def piece(h):
            return pl.ds(core * (TILES // 2) + h * PART + z * (PART // 4) + y * (PART // 16), PART // 16)

        def pieces(h):
            return pl.ds(core * (TILES // 2) + h * PART + z * (PART // 4), PART // 4)

        def last_copy(h):
            block = q_all.at[tiles(core, h)]
            return remote(block, block, qc_send.at[h], qc_recv.at[h], other)

        @stage_at("h")
        def _():
            for h in range(PARTS):
                landed_at("x", 2, h, lambda i: b_x.at[h, x])
                q_all[piece(h)] = (b_x[h, 0] + b_x[h, 1]) + (b_x[h, 2] + b_x[h, 3])
                for i, who in enumerate(ring["y"]):
                    block = q_all.at[piece(h)]
                    remote(block, block, rs_send.at[3, h, i], rs_recv.at[3, h, i], who).start()

        @stage_at("i")
        def _():
            for h in range(PARTS):
                landed_at("y", 3, h, lambda i: q_all.at[piece(h)])
                for i, who in enumerate(ring["z"]):
                    block = q_all.at[pieces(h)]
                    remote(block, block, rs_send.at[4, h, i], rs_recv.at[4, h, i], who).start()

        @stage_at("j")
        def _():
            for h in range(PARTS):
                landed_at("z", 4, h, lambda i: q_all.at[pieces(h)])
                last_copy(h).start()

        @stage_at("k")
        def _():
            for h in range(PARTS):
                last_copy(h).wait()

        @pl.when(s >= FINISH_FROM)
        def _():
            for i in range(FINISH_EACH):
                finish((s - FINISH_FROM) * FINISH_EACH + i)

        return carry

    lax.fori_loop(0, STEPS, step, 0)

    def rest(k, carry):
        finish(k)
        return carry

    lax.fori_loop(DONE, NC, rest, 0)
    gin_out[...] = gin[...].astype(BF16)

    own_copy.wait_send()
    for flow in range(7):
        block = g.at[:, pl.ds(0, OWN)]
        remote(block, block, bulk_send.at[flow], bulk_recv.at[flow, 0], other).wait_send()
    block = g.at[:, pl.ds(0, 7 * OWN)]
    remote(block, block, core_send.at[0], core_recv.at[0], other).wait_send()


def copy_out(*refs):
    sources, targets, sem = refs[:4], refs[4:8], refs[8]
    copies = [pltpu.make_async_copy(a, b, sem.at[i]) for i, (a, b) in enumerate(zip(sources, targets))]
    for c in copies:
        c.start()
    for c in copies:
        c.wait()


def shards(acts, grad_out, weight, residue, start_q):
    vmem, dma = pltpu.VMEM, pltpu.SemaphoreType.DMA
    hbm = pl.BlockSpec(memory_space=pl.ANY)
    here = pl.BlockSpec(memory_space=pltpu.VMEM)
    flops = 4 * TOK * FEAT * D_OUT
    results = pl.pallas_call(
        kernel,
        out_shape=[
            vmem((TOK, FEAT), BF16),
            vmem((RANK, FEAT), F32),
            vmem((RANK, D_OUT), F32),
            vmem((FEAT, D_OUT), BF16),
        ],
        in_specs=[hbm] * 5,
        out_specs=[here] * 4,
        scratch_shapes=[
            vmem((NC, TOK, CW), BF16),
            vmem((FEAT, D_OUT), BF16),
            vmem((NC, FEAT, CW), F32),
            vmem((FEAT, TOK), BF16),
            vmem((TOK, FEAT), F32),
            vmem((3 * RANK, D_OUT), BF16),
            vmem((8, RANK, 128), F32),
            vmem((3 * RANK, TOK), BF16),
            vmem((RANK, FEAT), F32),
            vmem((4, RANK, FEAT), F32),
            vmem((2, RANK, FEAT), F32),
            vmem((RANK, FEAT), F32),
            vmem((3 * RANK, FEAT), BF16),
            vmem((8, RANK, 128), F32),
            vmem((8, RANK, 128), F32),
            vmem((8, 8, 128), F32),
            vmem((2, 8, 128), F32),
            vmem((RANK, 128), F32),
            vmem((RANK, 128), F32),
            vmem((RANK, 6 * RANK), BF16),
            vmem((TILES, 8, 128), F32),
            vmem((PARTS, PART, 8, 128), F32),
            vmem((PARTS, 3, PART // 4, 8, 128), F32),
            vmem((PARTS, PART // 4, 8, 128), F32),
            vmem((PARTS, 3, PART // 16, 8, 128), F32),
            vmem((PARTS, 4, PART // 16, 8, 128), F32),
            vmem((TILES, 8, 128), F32),
            vmem((RANK, CW), F32),
            vmem((6 * RANK, CW), BF16),
            vmem((FEAT, 6 * RANK), BF16),
            dma((5,)),
            dma((7,)),
            dma((7, NC)),
            dma((1,)),
            dma((NC,)),
            dma((2,)),
            dma((7,)),
            dma((7,)),
            dma((7,)),
            dma((7,)),
            dma((7,)),
            dma((7,)),
            dma((1, 3)),
            dma((1, 3)),
            dma((3,)),
            dma((3,)),
            dma((PARTS,)),
            dma((PARTS,)),
            dma((5, PARTS, 3)),
            dma((5, PARTS, 3)),
            dma((PARTS,)),
            dma((PARTS,)),
        ],
        compiler_params=pltpu.CompilerParams(
            collective_id=1, has_side_effects=True, vmem_limit_bytes=46 * 2**20
        ),
        cost_estimate=pl.CostEstimate(flops=flops, bytes_accessed=24 * 2**20, transcendentals=0),
        name="gather_and_compress",
    )(*(pltpu.with_memory_space_constraint(a, pltpu.HBM) for a in (acts, grad_out, weight, residue[0], start_q.T)))
    grad_in, p_t, q_t, new = pl.pallas_call(
        copy_out,
        out_shape=[jax.ShapeDtypeStruct(r.shape, r.dtype) for r in results],
        in_specs=[here] * 4,
        out_specs=[hbm] * 4,
        scratch_shapes=[dma((4,))],
        compiler_params=pltpu.CompilerParams(vmem_limit_bytes=4 * 2**20),
        name="copy_out",
    )(*(pltpu.with_memory_space_constraint(r, pltpu.VMEM) for r in results))
    return grad_in, p_t.T, q_t.T, new[None]


def solution(mesh):
    in_specs = (
        P("dp", "tensor"),
        P(("dp", "tensor"), None),
        P("tensor", None),
        P("dp", "tensor", None),
        P(),
    )
    out_specs = (P("dp", "tensor"), P("tensor", None), P(), P("dp", "tensor", None))
    return jax.shard_map(shards, mesh=mesh, in_specs=in_specs, out_specs=out_specs, check_vma=False)
```

```python
import math

import jax
import jax.numpy as jnp
from jax import lax
from jax.experimental import pallas as pl
from jax.experimental.pallas import tpu as pltpu
from jax.sharding import PartitionSpec as P

MESH = pl.DeviceIdType.MESH
F32, BF16 = jnp.float32, jnp.bfloat16

D_IN, D_OUT, RANK, REPLICAS = 8192, 6144, 32, 8
TOK, FEAT, OWN = 1024, 512, 64
CW = 512
NC = D_OUT // CW
NT = (((1,), (1,)), ((), ()))

STAGE_AT = dict(a=1, b=3, c=5, d=7, e=9, f=9, g=10, h=11, i=12, j=13, k=14)
PARTS = 3
TILES = D_OUT // 128 * RANK // 8
PART = TILES // 2 // PARTS
STEPS = NC + 7
EARLY = 3


def place():
    d, t = lax.axis_index("dp"), lax.axis_index("tensor")
    return dict(y_lo=d // 4, z=d % 4, x=t // 4, y_hi=(t // 2) % 2, core=t % 2)


def device(at, **moved):
    q = {**at, **moved}
    return {"dp": q["y_lo"] * 4 + q["z"], "tensor": q["x"] * 4 + q["y_hi"] * 2 + q["core"]}


def along_y(at, by):
    y = (at["y_hi"] * 2 + at["y_lo"] + by) % 4
    return device(at, y_hi=y // 2, y_lo=y % 2)


def split3(v):
    hi = v.astype(BF16)
    rest = v - hi.astype(F32)
    mid = rest.astype(BF16)
    low = (rest - mid.astype(F32)).astype(BF16)
    return hi, mid, low


def rows3(v):
    return jnp.concatenate(split3(v), axis=0)


def sum3(v):
    n = v.shape[0] // 3
    return v[:n] + (v[n : 2 * n] + v[2 * n :])


def stack6(v):
    h, m, low = split3(v)
    return jnp.concatenate([h, m, h, low, h, m], axis=0)


def dot(a, b, dims=(((1,), (0,)), ((), ()))):
    return lax.dot_general(a, b, dims, preferred_element_type=F32)


def kernel(
    acts_hbm, grad_hbm, weight_hbm, residue_hbm, qt_hbm,
    gin_out, pt_ref, q_out, merged, i6, p6,
    g, pair_g, weight, residue, acts_t, gin, qt,
    qt3, gq_half, gq, gq3, part, ska_z, ska_y, skb_y, skb_z, st, st3, z_out, z_in, gram_in, gram_core, gram_all, linv,
    b_own, b_core, b_z, piece_z, b_y, b_x, q_all,
    load_sem, bulk_send, bulk_recv, core_send, core_recv, own_sem,
    gq_send, gq_recv, z_send, z_recv, gr_send, gr_recv, ring_send, ring_recv, pair_send, pair_recv,
    bc_send, bc_recv, rs_send, rs_recv, qc_send, qc_recv,
):
    acts = gin_out
    at = place()
    x, y_hi, y_lo, z, core = at["x"], at["y_hi"], at["y_lo"], at["z"], at["core"]
    y = y_hi * 2 + y_lo
    me = x * 4 + y_hi * 2 + core
    chip = x * 2 + y_hi
    other = device(at, core=1 - core)
    peers = [(dx, dy) for dx in range(4) for dy in range(2) if (dx, dy) != (0, 0)]
    peer_ids = [device(at, x=(x + dx) % 4, y_hi=(y_hi + dy) % 2) for dx, dy in peers]
    ring = {
        "x": [device(at, x=(x + i) % 4) for i in (1, 2, 3)],
        "y": [along_y(at, i) for i in (1, 2, 3)],
        "z": [device(at, z=(z + i) % 4) for i in (1, 2, 3)],
    }

    def chip_at(dx, dy):
        return ((x + dx + 4) % 4) * 2 + (y_hi + dy) % 2

    beyond, over = chip_at(2, 0), chip_at(0, 1)

    def chunk(k):
        return pl.ds(pl.multiple_of(k * CW, CW), CW)

    for k in range(NC):
        own = grad_hbm.at[:, pl.ds(k * CW, CW)]
        pltpu.make_async_copy(own, pair_g.at[k, core], load_sem.at[0]).start()
        pltpu.make_async_copy(own, g.at[k, chip, core], load_sem.at[5]).start()
    load_q = pltpu.make_async_copy(qt_hbm, qt, load_sem.at[1])
    load_res = pltpu.make_async_copy(residue_hbm, residue, load_sem.at[2])
    load_acts = pltpu.make_async_copy(acts_hbm, acts, load_sem.at[3])
    load_w = pltpu.make_async_copy(weight_hbm, weight, load_sem.at[4])
    load_q.start()
    load_acts.start()
    load_res.start()
    load_w.start()

    barrier = pltpu.get_barrier_semaphore()
    greet = [*peer_ids, other, ring["y"][0], ring["y"][2], *ring["z"]]
    for who in greet:
        pl.semaphore_signal(barrier, inc=1, device_id=who, device_id_type=MESH)
    load_q.wait()
    qt3[...] = rows3(qt[...])
    pltpu.make_async_copy(pair_g.at[:, core], pair_g.at[:, core], load_sem.at[0]).wait()
    pltpu.make_async_copy(g.at[:, chip, core], g.at[:, chip, core], load_sem.at[5]).wait()
    total = jnp.zeros((3 * RANK, 2 * OWN), F32)
    for k in range(NC):
        twice = jnp.concatenate([pair_g[k, core], pair_g[k, core]], axis=0)
        total += dot(qt3[:, k * CW : (k + 1) * CW], twice, NT)
    lane = lax.broadcasted_iota(jnp.int32, (RANK, 2 * OWN), 1)
    gq_half[core] = jnp.where(lane // OWN == core, sum3(total), 0.0)
    pl.semaphore_wait(barrier, len(greet))

    def remote(src, dst, send, recv, who):
        return pltpu.make_async_remote_copy(
            src_ref=src, dst_ref=dst, send_sem=send, recv_sem=recv, device_id=who, device_id_type=MESH
        )

    def bulk(flow, k, source, who):
        block = g.at[k, source, core]
        return remote(block, block, bulk_send.at[flow], bulk_recv.at[flow, k], who)

    def arrived(flow, k):
        bulk(flow, k, chip, other).wait_recv()

    def to_core(k):
        plane = g.at[k, :, core]
        return remote(plane, plane, core_send.at[0], core_recv.at[k], other)

    right, left, across = ring["x"][0], ring["x"][2], device(at, y_hi=1 - y_hi)

    own_copy = remote(pair_g.at[:, core], pair_g.at[:, core], own_sem.at[0], own_sem.at[1], other)
    half_copy = remote(gq_half.at[core], gq_half.at[core], own_sem.at[2], own_sem.at[3], other)
    half_copy.start()
    own_copy.start()

    def send_own(k):
        bulk(0, k, chip, right).start()
        bulk(1, k, chip, left).start()
        bulk(2, k, chip, across).start()

    def step(s, carry):
        @pl.when((s >= EARLY) & (s < NC))
        def _():
            send_own(s)

        @pl.when(s == 0)
        def _():
            send_own(0)
            half_copy.wait()
            gq[chip] = gq_half[0] + gq_half[1]
            for i, who in enumerate(peer_ids):
                remote(gq.at[chip], gq.at[chip], gq_send.at[i], gq_recv.at[i], who).start()
            for k in range(1, EARLY):
                send_own(k)
            load_res.wait()

            def add(k, total):
                return total + dot(qt3[:, chunk(k)], residue[:, chunk(k)], NT)

            part[...] = sum3(lax.fori_loop(0, NC, add, jnp.zeros((3 * RANK, FEAT), F32)))
            load_acts.wait()
            acts_t[...] = acts[...].T
            gin[...] = jnp.zeros_like(gin)

        @pl.when((s >= 2) & (s < NC + 2))
        def _():
            k = s - 2
            arrived(0, k)
            arrived(1, k)
            odd = k % 2
            ahead = device(at, x=(x + 1 + 2 * odd) % 4)
            bulk(3, k, chip_at(2 * odd - 1, 0), ahead).start()
            arrived(2, k)
            bulk(4, k, over, right).start()
            bulk(5, k, over, left).start()

        @pl.when((s >= 4) & (s < NC + 4))
        def _():
            k = s - 4
            arrived(3, k)
            bulk(6, k, beyond, across).start()
            arrived(4, k)
            arrived(5, k)

        @pl.when((s >= 6) & (s < NC + 6))
        def _():
            k = s - 6
            arrived(6, k)
            to_core(k).start()

        @pl.when(s == 4)
        def _():
            load_w.wait()

        @pl.when(s >= 7)
        def _():
            k = s - 7
            to_core(k).wait_recv()
            rows = g[k].reshape(TOK, CW)
            merged[k] = dot(acts_t[...], rows) + residue[:, chunk(k)].astype(F32)
            gin[...] += dot(rows, weight[:, chunk(k)], NT)

        def stage_at(name):
            return pl.when(s == STAGE_AT[name])

        def z_copies(ref, n):
            return [
                remote(ref.at[z], ref.at[z], ring_send.at[n, i], ring_recv.at[n, i], who)
                for i, who in enumerate(ring["z"])
            ]

        def y_copy(ref, n):
            near = device(at, y_lo=1 - y_lo)
            return remote(ref.at[y_lo], ref.at[y_lo], pair_send.at[n], pair_recv.at[n], near)

        @stage_at("a")
        def _():
            for i, who in enumerate(peer_ids):
                remote(gq.at[chip], gq.at[chip], gq_send.at[i], gq_recv.at[i], who).wait()
            for j in range(8):
                gq3[:, j * 128 : (j + 1) * 128] = rows3(gq[j])
            sketch = part[...] + sum3(dot(gq3[...], acts[...]))
            ska_z[z] = sketch[:, : FEAT // 2]
            skb_y[y_lo] = sketch[:, FEAT // 2 :]
            y_copy(skb_y, 0).start()
            for c in z_copies(ska_z, 0):
                c.start()

        @stage_at("b")
        def _():
            y_copy(skb_y, 0).wait()
            skb_z[z] = skb_y[0] + skb_y[1]
            for c in z_copies(skb_z, 1):
                c.start()
            for c in z_copies(ska_z, 0):
                c.wait()
            ska_y[y_lo] = (ska_z[0] + ska_z[1]) + (ska_z[2] + ska_z[3])
            y_copy(ska_y, 1).start()

        @stage_at("c")
        def _():
            y_copy(ska_y, 1).wait()
            for c in z_copies(skb_z, 1):
                c.wait()
            low = ska_y[0] + ska_y[1]
            high = (skb_z[0] + skb_z[1]) + (skb_z[2] + skb_z[3])
            sketch = jnp.concatenate([low, high], axis=1) * (1.0 / REPLICAS)
            st[...] = sketch
            st3[...] = rows3(sketch)
            zt = sum3(dot(st3[...], acts_t[...]))
            for j in range(8):
                z_out[j] = zt[:, j * 128 : (j + 1) * 128]
            for i, who in enumerate(peer_ids):
                dx, dy = peers[i]
                there = ((x + dx) % 4) * 2 + (y_hi + dy) % 2
                remote(z_out.at[there], z_in.at[chip], z_send.at[i], z_recv.at[i], who).start()
            z_in[chip] = z_out[chip]
            gram = lax.dot_general(
                sketch, sketch, NT, precision=lax.Precision.HIGHEST, preferred_element_type=F32
            )
            for i in range(4):
                gram_in[chip, :, i * RANK : (i + 1) * RANK] = gram[i * 8 : (i + 1) * 8]
            for i, who in enumerate(peer_ids):
                remote(gram_in.at[chip], gram_in.at[chip], gr_send.at[i], gr_recv.at[i], who).start()

            def from_residue(k, _):
                r = sum3(dot(st3[...], residue[:, chunk(k)]))
                for i in range(CW // 128):
                    b_own[pl.ds(k * (CW // 32) + 4 * i, 4)] = r[:, i * 128 : (i + 1) * 128].reshape(4, 8, 128)
                return 0

            lax.fori_loop(0, NC, from_residue, 0)

        def tiles(c, h):
            return pl.ds(c * (TILES // 2) + h * PART, PART)

        def fourth(i):
            return pl.ds(i * (PART // 4), PART // 4)

        def core_copy(h, start):
            c = remote(b_own.at[tiles(1 - core, h)], b_core.at[h], bc_send.at[h], bc_recv.at[h], other)
            c.start() if start else c.wait()

        @stage_at("d")
        def _():
            for i, who in enumerate(peer_ids):
                remote(z_out.at[0], z_in.at[0], z_send.at[i], z_recv.at[i], who).wait()
            total = z_in[0]
            for j in range(1, 8):
                total = total + z_in[j]
            z3 = rows3(total)
            own_copy.wait_recv()

            def from_grad(k, _):
                r = sum3(dot(z3, pair_g[k].reshape(2 * OWN, CW)))
                for i in range(CW // 128):
                    b_own[pl.ds(k * (CW // 32) + 4 * i, 4)] += r[:, i * 128 : (i + 1) * 128].reshape(4, 8, 128)
                return 0

            each = NC // 2 // PARTS
            first = (1 - core) * (NC // 2)
            for h in range(PARTS):
                lax.fori_loop(first + h * each, first + (h + 1) * each, from_grad, 0)
                core_copy(h, True)
            lax.fori_loop(core * (NC // 2), (core + 1) * (NC // 2), from_grad, 0)
            for i, who in enumerate(peer_ids):
                remote(gram_in.at[chip], gram_in.at[chip], gr_send.at[i], gr_recv.at[i], who).wait()
            total = gram_in[0]
            for j in range(1, 8):
                total = total + gram_in[j]
            gram_core[core] = total
            remote(gram_core.at[core], gram_core.at[core], pair_send.at[2], pair_recv.at[2], other).start()

            for h in range(PARTS):
                core_copy(h, False)
                b_core[h] += b_own[tiles(core, h)]
                for i, who in enumerate(ring["z"]):
                    there = fourth((z + i + 1) % 4)
                    remote(b_core.at[h, there], b_z.at[h, i], rs_send.at[0, h, i], rs_recv.at[0, h, i], who).start()
        @stage_at("e")
        def _():
            remote(gram_core.at[core], gram_core.at[core], pair_send.at[2], pair_recv.at[2], other).wait()
            packed = (gram_core[0] + gram_core[1]) * (1.0 / D_IN)
            gram_all[...] = jnp.zeros((RANK, 128), F32)
            for i in range(4):
                gram_all[i * 8 : (i + 1) * 8, 0:RANK] = packed[:, i * RANK : (i + 1) * RANK]
            sub = lax.broadcasted_iota(jnp.int32, (RANK, 128), 0)
            lane = lax.broadcasted_iota(jnp.int32, (RANK, 128), 1)
            unit = jnp.where(sub == lane, 1.0, 0.0).astype(F32)

            def eliminate(j, both):
                a, e = both
                row_a = jnp.sum(jnp.where(sub == j, a, 0.0), axis=0, keepdims=True)
                row_e = jnp.sum(jnp.where(sub == j, e, 0.0), axis=0, keepdims=True)
                col = jnp.sum(jnp.where(lane == j, a, 0.0), axis=1, keepdims=True)
                diag = jnp.sum(jnp.where(lane[0:1] == j, row_a, 0.0), axis=1, keepdims=True)
                scale = 1.0 / jnp.sqrt(diag)
                row_a, row_e = row_a * scale, row_e * scale
                factor = jnp.where(sub > j, col * scale, 0.0)
                a = jnp.where(sub == j, row_a, a - factor * row_a)
                e = jnp.where(sub == j, row_e, e - factor * row_e)
                return a, e

            linv[...] = lax.fori_loop(0, RANK, eliminate, (gram_all[...], unit))[1]
            ih, im, il = split3(linv[:, 0:RANK])
            i6[...] = jnp.concatenate([ih, ih, im, ih, il, im], axis=1)
            p_t = dot(i6[...], stack6(st[...]))
            pt_ref[...] = p_t
            ph, pm, pw = split3(p_t)
            p6[...] = jnp.concatenate([ph, ph, pm, ph, pw, pm], axis=0).T

        def landed_at(axis, stage, h, ref):
            for i, who in enumerate(ring[axis]):
                remote(ref(i), ref(i), rs_send.at[stage, h, i], rs_recv.at[stage, h, i], who).wait()

        @stage_at("f")
        def _():
            for h in range(PARTS):
                landed_at("z", 0, h, lambda i: b_z.at[h, i])
                piece_z[h] = (b_core[h, fourth(z)] + b_z[h, 0]) + (b_z[h, 1] + b_z[h, 2])
                for i, who in enumerate(ring["y"]):
                    there = pl.ds(((y + i + 1) % 4) * (PART // 16), PART // 16)
                    remote(piece_z.at[h, there], b_y.at[h, i], rs_send.at[1, h, i], rs_recv.at[1, h, i], who).start()

        @stage_at("g")
        def _():
            for h in range(PARTS):
                landed_at("y", 1, h, lambda i: b_y.at[h, i])
                own = piece_z[h, pl.ds(y * (PART // 16), PART // 16)]
                b_x[h, x] = (own + b_y[h, 0]) + (b_y[h, 1] + b_y[h, 2])
                for i, who in enumerate(ring["x"]):
                    block = b_x.at[h, x]
                    remote(block, block, rs_send.at[2, h, i], rs_recv.at[2, h, i], who).start()

        def piece(h):
            return pl.ds(core * (TILES // 2) + h * PART + z * (PART // 4) + y * (PART // 16), PART // 16)

        def pieces(h):
            return pl.ds(core * (TILES // 2) + h * PART + z * (PART // 4), PART // 4)

        def last_copy(h):
            block = q_all.at[tiles(core, h)]
            return remote(block, block, qc_send.at[h], qc_recv.at[h], other)

        @stage_at("h")
        def _():
            for h in range(PARTS):
                landed_at("x", 2, h, lambda i: b_x.at[h, x])
                q_all[piece(h)] = (b_x[h, 0] + b_x[h, 1]) + (b_x[h, 2] + b_x[h, 3])
                for i, who in enumerate(ring["y"]):
                    block = q_all.at[piece(h)]
                    remote(block, block, rs_send.at[3, h, i], rs_recv.at[3, h, i], who).start()

        @stage_at("i")
        def _():
            for h in range(PARTS):
                landed_at("y", 3, h, lambda i: q_all.at[piece(h)])
                for i, who in enumerate(ring["z"]):
                    block = q_all.at[pieces(h)]
                    remote(block, block, rs_send.at[4, h, i], rs_recv.at[4, h, i], who).start()

        @stage_at("j")
        def _():
            for h in range(PARTS):
                landed_at("z", 4, h, lambda i: q_all.at[pieces(h)])
                last_copy(h).start()

        @stage_at("k")
        def _():
            for h in range(PARTS):
                last_copy(h).wait()

        return carry

    lax.fori_loop(0, STEPS, step, 0)

    q_out[...] = q_all[...]
    gin_out[...] = gin[...].astype(BF16)

    own_copy.wait_send()
    for flow in range(7):
        block = g.at[:, 0, 0]
        remote(block, block, bulk_send.at[flow], bulk_recv.at[flow, 0], other).wait_send()
    block = g.at[:, :, core]
    remote(block, block, core_send.at[0], core_recv.at[0], other).wait_send()


def finish(
    gin, p_t, q_all, merged, i6, p6, gin_hbm, pt_hbm, qt_hbm, new_hbm, new, q_t, b_t, q6, sem
):
    store_gin = pltpu.make_async_copy(gin, gin_hbm, sem.at[0])
    store_p = pltpu.make_async_copy(p_t, pt_hbm, sem.at[1])
    store_gin.start()
    store_p.start()

    def body(k, carry):
        columns = pl.ds(pl.multiple_of(k * CW, CW), CW)
        for i in range(CW // 128):
            block = q_all[pl.ds(k * (CW // 32) + 4 * i, 4)]
            b_t[:, i * 128 : (i + 1) * 128] = block.reshape(RANK, 128)
        q = dot(i6[...], stack6(b_t[...])) * (1.0 / (REPLICAS * math.sqrt(D_IN)))
        q_t[:, columns] = q
        q6[...] = stack6(q * (1.0 / math.sqrt(D_IN)))
        new[k] = (merged[k] - dot(p6[...], q6[...])).astype(BF16)
        pltpu.make_async_copy(new.at[k], new_hbm.at[:, columns], sem.at[2]).start()
        return carry

    lax.fori_loop(0, NC, body, 0)
    store_q = pltpu.make_async_copy(q_t, qt_hbm, sem.at[3])
    store_q.start()
    pltpu.make_async_copy(new, new, sem.at[2]).wait()
    store_gin.wait()
    store_p.wait()
    store_q.wait()


def shards(acts, grad_out, weight, residue, start_q):
    vmem, dma = pltpu.VMEM, pltpu.SemaphoreType.DMA
    hbm = pl.BlockSpec(memory_space=pl.ANY)
    here = pl.BlockSpec(memory_space=pltpu.VMEM)
    flops = 4 * TOK * FEAT * D_OUT
    results = pl.pallas_call(
        kernel,
        out_shape=[
            vmem((TOK, FEAT), BF16),
            vmem((RANK, FEAT), F32),
            vmem((TILES, 8, 128), F32),
            vmem((NC, FEAT, CW), F32),
            vmem((RANK, 6 * RANK), BF16),
            vmem((FEAT, 6 * RANK), BF16),
        ],
        in_specs=[hbm] * 5,
        out_specs=[here] * 6,
        scratch_shapes=[
            vmem((NC, TOK // OWN // 2, 2, OWN, CW), BF16),
            vmem((NC, 2, OWN, CW), BF16),
            vmem((FEAT, D_OUT), BF16),
            vmem((FEAT, D_OUT), BF16),
            vmem((FEAT, TOK), BF16),
            vmem((TOK, FEAT), F32),
            vmem((RANK, D_OUT), F32),
            vmem((3 * RANK, D_OUT), BF16),
            vmem((2, RANK, 128), F32),
            vmem((8, RANK, 128), F32),
            vmem((3 * RANK, TOK), BF16),
            vmem((RANK, FEAT), F32),
            vmem((4, RANK, FEAT // 2), F32),
            vmem((2, RANK, FEAT // 2), F32),
            vmem((2, RANK, FEAT // 2), F32),
            vmem((4, RANK, FEAT // 2), F32),
            vmem((RANK, FEAT), F32),
            vmem((3 * RANK, FEAT), BF16),
            vmem((8, RANK, 128), F32),
            vmem((8, RANK, 128), F32),
            vmem((8, 8, 128), F32),
            vmem((2, 8, 128), F32),
            vmem((RANK, 128), F32),
            vmem((RANK, 128), F32),
            vmem((TILES, 8, 128), F32),
            vmem((PARTS, PART, 8, 128), F32),
            vmem((PARTS, 3, PART // 4, 8, 128), F32),
            vmem((PARTS, PART // 4, 8, 128), F32),
            vmem((PARTS, 3, PART // 16, 8, 128), F32),
            vmem((PARTS, 4, PART // 16, 8, 128), F32),
            vmem((TILES, 8, 128), F32),
            dma((6,)),
            dma((7,)),
            dma((7, NC)),
            dma((1,)),
            dma((NC,)),
            dma((4,)),
            dma((7,)),
            dma((7,)),
            dma((7,)),
            dma((7,)),
            dma((7,)),
            dma((7,)),
            dma((2, 3)),
            dma((2, 3)),
            dma((3,)),
            dma((3,)),
            dma((PARTS,)),
            dma((PARTS,)),
            dma((5, PARTS, 3)),
            dma((5, PARTS, 3)),
            dma((PARTS,)),
            dma((PARTS,)),
        ],
        compiler_params=pltpu.CompilerParams(
            collective_id=1, has_side_effects=True, vmem_limit_bytes=40 * 2**20
        ),
        cost_estimate=pl.CostEstimate(flops=flops, bytes_accessed=24 * 2**20, transcendentals=0),
        name="gather_and_compress",
    )(*(pltpu.with_memory_space_constraint(a, pltpu.HBM) for a in (acts, grad_out, weight, residue[0], start_q.T)))
    grad_in, p_t, q_t, new = pl.pallas_call(
        finish,
        out_shape=[
            jax.ShapeDtypeStruct((TOK, FEAT), BF16),
            jax.ShapeDtypeStruct((RANK, FEAT), F32),
            jax.ShapeDtypeStruct((RANK, D_OUT), F32),
            jax.ShapeDtypeStruct((FEAT, D_OUT), BF16),
        ],
        in_specs=[here] * 6,
        out_specs=[hbm] * 4,
        scratch_shapes=[
            vmem((NC, FEAT, CW), BF16),
            vmem((RANK, D_OUT), F32),
            vmem((RANK, CW), F32),
            vmem((6 * RANK, CW), BF16),
            dma((4,)),
        ],
        compiler_params=pltpu.CompilerParams(vmem_limit_bytes=14 * 2**20),
        name="finish",
    )(*(pltpu.with_memory_space_constraint(r, pltpu.VMEM) for r in results))
    return grad_in, p_t.T, q_t.T, new[None]


def solution(mesh):
    in_specs = (
        P("dp", "tensor"),
        P(("dp", "tensor"), None),
        P("tensor", None),
        P("dp", "tensor", None),
        P(),
    )
    out_specs = (P("dp", "tensor"), P("tensor", None), P(), P("dp", "tensor", None))
    return jax.shard_map(shards, mesh=mesh, in_specs=in_specs, out_specs=out_specs, check_vma=False)
```

```python
import math

import jax
import jax.numpy as jnp
from jax import lax
from jax.experimental import pallas as pl
from jax.experimental.pallas import tpu as pltpu
from jax.sharding import PartitionSpec as P

MESH = pl.DeviceIdType.MESH
F32, BF16 = jnp.float32, jnp.bfloat16

D_IN, D_OUT, RANK, REPLICAS = 8192, 6144, 32, 8
TOK, FEAT, OWN = 1024, 512, 64
CW = 512
NC = D_OUT // CW
NT = (((1,), (1,)), ((), ()))

STAGE_AT = dict(a=1, b=3, c=5, d=7, e=9, f=9, g=10, h=11, i=12, j=13, k=14)
PARTS = 3
TILES = D_OUT // 128 * RANK // 8
PART = TILES // 2 // PARTS
STEPS = NC + 7
WIDE = 3072
EARLY = 3


def place():
    d, t = lax.axis_index("dp"), lax.axis_index("tensor")
    return dict(y_lo=d // 4, z=d % 4, x=t // 4, y_hi=(t // 2) % 2, core=t % 2)


def device(at, **moved):
    q = {**at, **moved}
    return {"dp": q["y_lo"] * 4 + q["z"], "tensor": q["x"] * 4 + q["y_hi"] * 2 + q["core"]}


def along_y(at, by):
    y = (at["y_hi"] * 2 + at["y_lo"] + by) % 4
    return device(at, y_hi=y // 2, y_lo=y % 2)


def split3(v):
    hi = v.astype(BF16)
    rest = v - hi.astype(F32)
    mid = rest.astype(BF16)
    low = (rest - mid.astype(F32)).astype(BF16)
    return hi, mid, low


def rows3(v):
    return jnp.concatenate(split3(v), axis=0)


def sum3(v):
    n = v.shape[0] // 3
    return v[:n] + (v[n : 2 * n] + v[2 * n :])


def stack6(v):
    h, m, low = split3(v)
    return jnp.concatenate([h, m, h, low, h, m], axis=0)


def dot(a, b, dims=(((1,), (0,)), ((), ()))):
    return lax.dot_general(a, b, dims, preferred_element_type=F32)


def kernel(
    acts_hbm, grad_hbm, weight_hbm, residue_hbm, qt_hbm,
    gin_out, pt_ref, q_out, merged, i6, p6,
    g, pair_g, weight, residue, acts_t, gin, qt,
    qt3, gq_half, gq, gq3, part, ska_z, ska_y, skb_y, skb_z, st, st3, z_out, z_in, gram_in, gram_core, gram_all, linv,
    b_own, b_core, b_z, piece_z, b_y, b_x, q_all,
    load_sem, bulk_send, bulk_recv, core_send, core_recv, own_sem,
    gq_send, gq_recv, z_send, z_recv, gr_send, gr_recv, ring_send, ring_recv, pair_send, pair_recv,
    bc_send, bc_recv, rs_send, rs_recv, qc_send, qc_recv,
):
    acts = gin_out
    at = place()
    x, y_hi, y_lo, z, core = at["x"], at["y_hi"], at["y_lo"], at["z"], at["core"]
    y = y_hi * 2 + y_lo
    me = x * 4 + y_hi * 2 + core
    chip = x * 2 + y_hi
    other = device(at, core=1 - core)
    peers = [(dx, dy) for dx in range(4) for dy in range(2) if (dx, dy) != (0, 0)]
    peer_ids = [device(at, x=(x + dx) % 4, y_hi=(y_hi + dy) % 2) for dx, dy in peers]
    ring = {
        "x": [device(at, x=(x + i) % 4) for i in (1, 2, 3)],
        "y": [along_y(at, i) for i in (1, 2, 3)],
        "z": [device(at, z=(z + i) % 4) for i in (1, 2, 3)],
    }

    def chip_at(dx, dy):
        return ((x + dx + 4) % 4) * 2 + (y_hi + dy) % 2

    beyond, over = chip_at(2, 0), chip_at(0, 1)

    def chunk(k):
        return pl.ds(pl.multiple_of(k * CW, CW), CW)

    for k in range(NC):
        own = grad_hbm.at[:, pl.ds(k * CW, CW)]
        pltpu.make_async_copy(own, pair_g.at[k, core], load_sem.at[0]).start()
        pltpu.make_async_copy(own, g.at[k, chip, core], load_sem.at[5]).start()
    load_q = pltpu.make_async_copy(qt_hbm, qt, load_sem.at[1])
    load_res = pltpu.make_async_copy(residue_hbm, residue, load_sem.at[2])
    load_acts = pltpu.make_async_copy(acts_hbm, acts, load_sem.at[3])
    load_w = pltpu.make_async_copy(weight_hbm, weight, load_sem.at[4])
    load_q.start()
    load_acts.start()
    load_res.start()
    load_w.start()

    barrier = pltpu.get_barrier_semaphore()
    greet = [*peer_ids, other, ring["y"][0], ring["y"][2], *ring["z"]]
    for who in greet:
        pl.semaphore_signal(barrier, inc=1, device_id=who, device_id_type=MESH)
    load_q.wait()
    qt3[...] = rows3(qt[...])
    pltpu.make_async_copy(pair_g.at[:, core], pair_g.at[:, core], load_sem.at[0]).wait()
    pltpu.make_async_copy(g.at[:, chip, core], g.at[:, chip, core], load_sem.at[5]).wait()
    total = jnp.zeros((3 * RANK, 2 * OWN), F32)
    for k in range(NC):
        twice = jnp.concatenate([pair_g[k, core], pair_g[k, core]], axis=0)
        total += dot(qt3[:, k * CW : (k + 1) * CW], twice, NT)
    lane = lax.broadcasted_iota(jnp.int32, (RANK, 2 * OWN), 1)
    gq_half[core] = jnp.where(lane // OWN == core, sum3(total), 0.0)
    pl.semaphore_wait(barrier, len(greet))

    def remote(src, dst, send, recv, who):
        return pltpu.make_async_remote_copy(
            src_ref=src, dst_ref=dst, send_sem=send, recv_sem=recv, device_id=who, device_id_type=MESH
        )

    def bulk(flow, k, source, who):
        block = g.at[k, source, core]
        return remote(block, block, bulk_send.at[flow], bulk_recv.at[flow, k], who)

    def arrived(flow, k):
        bulk(flow, k, chip, other).wait_recv()

    def to_core(k):
        plane = g.at[k, :, core]
        return remote(plane, plane, core_send.at[0], core_recv.at[k], other)

    right, left, across = ring["x"][0], ring["x"][2], device(at, y_hi=1 - y_hi)

    own_copy = remote(pair_g.at[:, core], pair_g.at[:, core], own_sem.at[0], own_sem.at[1], other)
    half_copy = remote(gq_half.at[core], gq_half.at[core], own_sem.at[2], own_sem.at[3], other)
    half_copy.start()
    own_copy.start()

    def send_own(k):
        bulk(0, k, chip, right).start()
        bulk(1, k, chip, left).start()
        bulk(2, k, chip, across).start()

    def step(s, carry):
        @pl.when((s >= EARLY) & (s < NC))
        def _():
            send_own(s)

        @pl.when(s == 0)
        def _():
            send_own(0)
            half_copy.wait()
            gq[chip] = gq_half[0] + gq_half[1]
            for i, who in enumerate(peer_ids):
                remote(gq.at[chip], gq.at[chip], gq_send.at[i], gq_recv.at[i], who).start()
            for k in range(1, EARLY):
                send_own(k)
            load_res.wait()

            def add(k, total):
                return total + dot(qt3[:, chunk(k)], residue[:, chunk(k)], NT)

            part[...] = sum3(lax.fori_loop(0, NC, add, jnp.zeros((3 * RANK, FEAT), F32)))
            load_acts.wait()
            acts_t[...] = acts[...].T
            gin[...] = jnp.zeros_like(gin)

        @pl.when((s >= 2) & (s < NC + 2))
        def _():
            k = s - 2
            arrived(0, k)
            arrived(1, k)
            odd = k % 2
            ahead = device(at, x=(x + 1 + 2 * odd) % 4)
            bulk(3, k, chip_at(2 * odd - 1, 0), ahead).start()
            arrived(2, k)
            bulk(4, k, over, right).start()
            bulk(5, k, over, left).start()

        @pl.when((s >= 4) & (s < NC + 4))
        def _():
            k = s - 4
            arrived(3, k)
            bulk(6, k, beyond, across).start()
            arrived(4, k)
            arrived(5, k)

        @pl.when((s >= 6) & (s < NC + 6))
        def _():
            k = s - 6
            arrived(6, k)
            to_core(k).start()

        @pl.when(s == 4)
        def _():
            load_w.wait()

        @pl.when(s >= 7)
        def _():
            k = s - 7
            to_core(k).wait_recv()
            rows = g[k].reshape(TOK, CW)
            merged[k] = dot(acts_t[...], rows) + residue[:, chunk(k)].astype(F32)
            gin[...] += dot(rows, weight[:, chunk(k)], NT)

        def stage_at(name):
            return pl.when(s == STAGE_AT[name])

        def z_copies(ref, n):
            return [
                remote(ref.at[z], ref.at[z], ring_send.at[n, i], ring_recv.at[n, i], who)
                for i, who in enumerate(ring["z"])
            ]

        def y_copy(ref, n):
            near = device(at, y_lo=1 - y_lo)
            return remote(ref.at[y_lo], ref.at[y_lo], pair_send.at[n], pair_recv.at[n], near)

        @stage_at("a")
        def _():
            for i, who in enumerate(peer_ids):
                remote(gq.at[chip], gq.at[chip], gq_send.at[i], gq_recv.at[i], who).wait()
            for j in range(8):
                gq3[:, j * 128 : (j + 1) * 128] = rows3(gq[j])
            sketch = part[...] + sum3(dot(gq3[...], acts[...]))
            ska_z[z] = sketch[:, : FEAT // 2]
            skb_y[y_lo] = sketch[:, FEAT // 2 :]
            y_copy(skb_y, 0).start()
            for c in z_copies(ska_z, 0):
                c.start()

        @stage_at("b")
        def _():
            y_copy(skb_y, 0).wait()
            skb_z[z] = skb_y[0] + skb_y[1]
            for c in z_copies(skb_z, 1):
                c.start()
            for c in z_copies(ska_z, 0):
                c.wait()
            ska_y[y_lo] = (ska_z[0] + ska_z[1]) + (ska_z[2] + ska_z[3])
            y_copy(ska_y, 1).start()

        @stage_at("c")
        def _():
            y_copy(ska_y, 1).wait()
            for c in z_copies(skb_z, 1):
                c.wait()
            low = ska_y[0] + ska_y[1]
            high = (skb_z[0] + skb_z[1]) + (skb_z[2] + skb_z[3])
            sketch = jnp.concatenate([low, high], axis=1) * (1.0 / REPLICAS)
            st[...] = sketch
            st3[...] = rows3(sketch)
            zt = sum3(dot(st3[...], acts_t[...]))
            for j in range(8):
                z_out[j] = zt[:, j * 128 : (j + 1) * 128]
            for i, who in enumerate(peer_ids):
                dx, dy = peers[i]
                there = ((x + dx) % 4) * 2 + (y_hi + dy) % 2
                remote(z_out.at[there], z_in.at[chip], z_send.at[i], z_recv.at[i], who).start()
            z_in[chip] = z_out[chip]
            gram = lax.dot_general(
                sketch, sketch, NT, precision=lax.Precision.HIGHEST, preferred_element_type=F32
            )
            for i in range(4):
                gram_in[chip, :, i * RANK : (i + 1) * RANK] = gram[i * 8 : (i + 1) * 8]
            for i, who in enumerate(peer_ids):
                remote(gram_in.at[chip], gram_in.at[chip], gr_send.at[i], gr_recv.at[i], who).start()

            def from_residue(k, _):
                r = sum3(dot(st3[...], residue[:, chunk(k)]))
                for i in range(CW // 128):
                    b_own[pl.ds(k * (CW // 32) + 4 * i, 4)] = r[:, i * 128 : (i + 1) * 128].reshape(4, 8, 128)
                return 0

            lax.fori_loop(0, NC, from_residue, 0)

        def tiles(c, h):
            return pl.ds(c * (TILES // 2) + h * PART, PART)

        def fourth(i):
            return pl.ds(i * (PART // 4), PART // 4)

        def core_copy(h, start):
            c = remote(b_own.at[tiles(1 - core, h)], b_core.at[h], bc_send.at[h], bc_recv.at[h], other)
            c.start() if start else c.wait()

        @stage_at("d")
        def _():
            for i, who in enumerate(peer_ids):
                remote(z_out.at[0], z_in.at[0], z_send.at[i], z_recv.at[i], who).wait()
            total = z_in[0]
            for j in range(1, 8):
                total = total + z_in[j]
            z3 = rows3(total)
            own_copy.wait_recv()

            def from_grad(k, _):
                r = sum3(dot(z3, pair_g[k].reshape(2 * OWN, CW)))
                for i in range(CW // 128):
                    b_own[pl.ds(k * (CW // 32) + 4 * i, 4)] += r[:, i * 128 : (i + 1) * 128].reshape(4, 8, 128)
                return 0

            each = NC // 2 // PARTS
            first = (1 - core) * (NC // 2)
            for h in range(PARTS):
                lax.fori_loop(first + h * each, first + (h + 1) * each, from_grad, 0)
                core_copy(h, True)
            lax.fori_loop(core * (NC // 2), (core + 1) * (NC // 2), from_grad, 0)
            for i, who in enumerate(peer_ids):
                remote(gram_in.at[chip], gram_in.at[chip], gr_send.at[i], gr_recv.at[i], who).wait()
            total = gram_in[0]
            for j in range(1, 8):
                total = total + gram_in[j]
            gram_core[core] = total
            remote(gram_core.at[core], gram_core.at[core], pair_send.at[2], pair_recv.at[2], other).start()

            for h in range(PARTS):
                core_copy(h, False)
                b_core[h] += b_own[tiles(core, h)]
                for i, who in enumerate(ring["z"]):
                    there = fourth((z + i + 1) % 4)
                    remote(b_core.at[h, there], b_z.at[h, i], rs_send.at[0, h, i], rs_recv.at[0, h, i], who).start()
        @stage_at("e")
        def _():
            remote(gram_core.at[core], gram_core.at[core], pair_send.at[2], pair_recv.at[2], other).wait()
            packed = (gram_core[0] + gram_core[1]) * (1.0 / D_IN)
            gram_all[...] = jnp.zeros((RANK, 128), F32)
            for i in range(4):
                gram_all[i * 8 : (i + 1) * 8, 0:RANK] = packed[:, i * RANK : (i + 1) * RANK]
            sub = lax.broadcasted_iota(jnp.int32, (RANK, 128), 0)
            lane = lax.broadcasted_iota(jnp.int32, (RANK, 128), 1)
            unit = jnp.where(sub == lane, 1.0, 0.0).astype(F32)

            def eliminate(j, both):
                a, e = both
                row_a = jnp.sum(jnp.where(sub == j, a, 0.0), axis=0, keepdims=True)
                row_e = jnp.sum(jnp.where(sub == j, e, 0.0), axis=0, keepdims=True)
                col = jnp.sum(jnp.where(lane == j, a, 0.0), axis=1, keepdims=True)
                diag = jnp.sum(jnp.where(lane[0:1] == j, row_a, 0.0), axis=1, keepdims=True)
                scale = 1.0 / jnp.sqrt(diag)
                row_a, row_e = row_a * scale, row_e * scale
                factor = jnp.where(sub > j, col * scale, 0.0)
                a = jnp.where(sub == j, row_a, a - factor * row_a)
                e = jnp.where(sub == j, row_e, e - factor * row_e)
                return a, e

            linv[...] = lax.fori_loop(0, RANK, eliminate, (gram_all[...], unit))[1]
            ih, im, il = split3(linv[:, 0:RANK])
            i6[...] = jnp.concatenate([ih, ih, im, ih, il, im], axis=1)
            p_t = dot(i6[...], stack6(st[...]))
            pt_ref[...] = p_t
            ph, pm, pw = split3(p_t)
            p6[...] = jnp.concatenate([ph, ph, pm, ph, pw, pm], axis=0).T

        def landed_at(axis, stage, h, ref):
            for i, who in enumerate(ring[axis]):
                remote(ref(i), ref(i), rs_send.at[stage, h, i], rs_recv.at[stage, h, i], who).wait()

        @stage_at("f")
        def _():
            for h in range(PARTS):
                landed_at("z", 0, h, lambda i: b_z.at[h, i])
                piece_z[h] = (b_core[h, fourth(z)] + b_z[h, 0]) + (b_z[h, 1] + b_z[h, 2])
                for i, who in enumerate(ring["y"]):
                    there = pl.ds(((y + i + 1) % 4) * (PART // 16), PART // 16)
                    remote(piece_z.at[h, there], b_y.at[h, i], rs_send.at[1, h, i], rs_recv.at[1, h, i], who).start()

        @stage_at("g")
        def _():
            for h in range(PARTS):
                landed_at("y", 1, h, lambda i: b_y.at[h, i])
                own = piece_z[h, pl.ds(y * (PART // 16), PART // 16)]
                b_x[h, x] = (own + b_y[h, 0]) + (b_y[h, 1] + b_y[h, 2])
                for i, who in enumerate(ring["x"]):
                    block = b_x.at[h, x]
                    remote(block, block, rs_send.at[2, h, i], rs_recv.at[2, h, i], who).start()

        def piece(h):
            return pl.ds(core * (TILES // 2) + h * PART + z * (PART // 4) + y * (PART // 16), PART // 16)

        def pieces(h):
            return pl.ds(core * (TILES // 2) + h * PART + z * (PART // 4), PART // 4)

        def last_copy(h):
            block = q_all.at[tiles(core, h)]
            return remote(block, block, qc_send.at[h], qc_recv.at[h], other)

        @stage_at("h")
        def _():
            for h in range(PARTS):
                landed_at("x", 2, h, lambda i: b_x.at[h, x])
                q_all[piece(h)] = (b_x[h, 0] + b_x[h, 1]) + (b_x[h, 2] + b_x[h, 3])
                for i, who in enumerate(ring["y"]):
                    block = q_all.at[piece(h)]
                    remote(block, block, rs_send.at[3, h, i], rs_recv.at[3, h, i], who).start()

        @stage_at("i")
        def _():
            for h in range(PARTS):
                landed_at("y", 3, h, lambda i: q_all.at[piece(h)])
                for i, who in enumerate(ring["z"]):
                    block = q_all.at[pieces(h)]
                    remote(block, block, rs_send.at[4, h, i], rs_recv.at[4, h, i], who).start()

        @stage_at("j")
        def _():
            for h in range(PARTS):
                landed_at("z", 4, h, lambda i: q_all.at[pieces(h)])
                last_copy(h).start()

        @stage_at("k")
        def _():
            for h in range(PARTS):
                last_copy(h).wait()

        return carry

    lax.fori_loop(0, STEPS, step, 0)

    q_out[...] = q_all[...]
    gin_out[...] = gin[...].astype(BF16)

    own_copy.wait_send()
    for flow in range(7):
        block = g.at[:, 0, 0]
        remote(block, block, bulk_send.at[flow], bulk_recv.at[flow, 0], other).wait_send()
    block = g.at[:, :, core]
    remote(block, block, core_send.at[0], core_recv.at[0], other).wait_send()


def finish(
    gin, p_t, q_all, merged, i6, p6, gin_hbm, pt_hbm, qt_hbm, new_hbm, new, q_t, b_t, q6, sem
):
    store_gin = pltpu.make_async_copy(gin, gin_hbm, sem.at[0])
    store_p = pltpu.make_async_copy(p_t, pt_hbm, sem.at[1])
    store_gin.start()
    store_p.start()

    def right(j, carry):
        columns = pl.ds(pl.multiple_of(j * WIDE, WIDE), WIDE)
        for i in range(WIDE // 128):
            block = q_all[pl.ds(j * (WIDE // 32) + 4 * i, 4)]
            b_t[:, i * 128 : (i + 1) * 128] = block.reshape(RANK, 128)
        q = dot(i6[...], stack6(b_t[...])) * (1.0 / (REPLICAS * math.sqrt(D_IN)))
        q_t[:, columns] = q
        q6[:, columns] = stack6(q * (1.0 / math.sqrt(D_IN)))
        return carry

    def body(k, carry):
        columns = pl.ds(pl.multiple_of(k * CW, CW), CW)
        new[k] = (merged[k] - dot(p6[...], q6[:, columns])).astype(BF16)
        pltpu.make_async_copy(new.at[k], new_hbm.at[:, columns], sem.at[2]).start()
        return carry

    lax.fori_loop(0, D_OUT // WIDE, right, 0)
    store_q = pltpu.make_async_copy(q_t, qt_hbm, sem.at[3])
    store_q.start()
    lax.fori_loop(0, NC, body, 0, unroll=3)
    pltpu.make_async_copy(new, new, sem.at[2]).wait()
    store_gin.wait()
    store_p.wait()
    store_q.wait()


def shards(acts, grad_out, weight, residue, start_q):
    vmem, dma = pltpu.VMEM, pltpu.SemaphoreType.DMA
    hbm = pl.BlockSpec(memory_space=pl.ANY)
    here = pl.BlockSpec(memory_space=pltpu.VMEM)
    flops = 4 * TOK * FEAT * D_OUT
    results = pl.pallas_call(
        kernel,
        out_shape=[
            vmem((TOK, FEAT), BF16),
            vmem((RANK, FEAT), F32),
            vmem((TILES, 8, 128), F32),
            vmem((NC, FEAT, CW), F32),
            vmem((RANK, 6 * RANK), BF16),
            vmem((FEAT, 6 * RANK), BF16),
        ],
        in_specs=[hbm] * 5,
        out_specs=[here] * 6,
        scratch_shapes=[
            vmem((NC, TOK // OWN // 2, 2, OWN, CW), BF16),
            vmem((NC, 2, OWN, CW), BF16),
            vmem((FEAT, D_OUT), BF16),
            vmem((FEAT, D_OUT), BF16),
            vmem((FEAT, TOK), BF16),
            vmem((TOK, FEAT), F32),
            vmem((RANK, D_OUT), F32),
            vmem((3 * RANK, D_OUT), BF16),
            vmem((2, RANK, 128), F32),
            vmem((8, RANK, 128), F32),
            vmem((3 * RANK, TOK), BF16),
            vmem((RANK, FEAT), F32),
            vmem((4, RANK, FEAT // 2), F32),
            vmem((2, RANK, FEAT // 2), F32),
            vmem((2, RANK, FEAT // 2), F32),
            vmem((4, RANK, FEAT // 2), F32),
            vmem((RANK, FEAT), F32),
            vmem((3 * RANK, FEAT), BF16),
            vmem((8, RANK, 128), F32),
            vmem((8, RANK, 128), F32),
            vmem((8, 8, 128), F32),
            vmem((2, 8, 128), F32),
            vmem((RANK, 128), F32),
            vmem((RANK, 128), F32),
            vmem((TILES, 8, 128), F32),
            vmem((PARTS, PART, 8, 128), F32),
            vmem((PARTS, 3, PART // 4, 8, 128), F32),
            vmem((PARTS, PART // 4, 8, 128), F32),
            vmem((PARTS, 3, PART // 16, 8, 128), F32),
            vmem((PARTS, 4, PART // 16, 8, 128), F32),
            vmem((TILES, 8, 128), F32),
            dma((6,)),
            dma((7,)),
            dma((7, NC)),
            dma((1,)),
            dma((NC,)),
            dma((4,)),
            dma((7,)),
            dma((7,)),
            dma((7,)),
            dma((7,)),
            dma((7,)),
            dma((7,)),
            dma((2, 3)),
            dma((2, 3)),
            dma((3,)),
            dma((3,)),
            dma((PARTS,)),
            dma((PARTS,)),
            dma((5, PARTS, 3)),
            dma((5, PARTS, 3)),
            dma((PARTS,)),
            dma((PARTS,)),
        ],
        compiler_params=pltpu.CompilerParams(
            collective_id=1, has_side_effects=True, vmem_limit_bytes=40 * 2**20
        ),
        cost_estimate=pl.CostEstimate(flops=flops, bytes_accessed=24 * 2**20, transcendentals=0),
        name="gather_and_compress",
    )(*(pltpu.with_memory_space_constraint(a, pltpu.HBM) for a in (acts, grad_out, weight, residue[0], start_q.T)))
    grad_in, p_t, q_t, new = pl.pallas_call(
        finish,
        out_shape=[
            jax.ShapeDtypeStruct((TOK, FEAT), BF16),
            jax.ShapeDtypeStruct((RANK, FEAT), F32),
            jax.ShapeDtypeStruct((RANK, D_OUT), F32),
            jax.ShapeDtypeStruct((FEAT, D_OUT), BF16),
        ],
        in_specs=[here] * 6,
        out_specs=[hbm] * 4,
        scratch_shapes=[
            vmem((NC, FEAT, CW), BF16),
            vmem((RANK, D_OUT), F32),
            vmem((RANK, WIDE), F32),
            vmem((6 * RANK, D_OUT), BF16),
            dma((4,)),
        ],
        compiler_params=pltpu.CompilerParams(vmem_limit_bytes=14 * 2**20),
        name="finish",
    )(*(pltpu.with_memory_space_constraint(r, pltpu.VMEM) for r in results))
    return grad_in, p_t.T, q_t.T, new[None]


def solution(mesh):
    in_specs = (
        P("dp", "tensor"),
        P(("dp", "tensor"), None),
        P("tensor", None),
        P("dp", "tensor", None),
        P(),
    )
    out_specs = (P("dp", "tensor"), P("tensor", None), P(), P("dp", "tensor", None))
    return jax.shard_map(shards, mesh=mesh, in_specs=in_specs, out_specs=out_specs, check_vma=False)
```

```python
import math

import jax
import jax.numpy as jnp
from jax import lax
from jax.experimental import pallas as pl
from jax.experimental.pallas import tpu as pltpu
from jax.sharding import PartitionSpec as P

MESH = pl.DeviceIdType.MESH
F32, BF16 = jnp.float32, jnp.bfloat16

D_IN, D_OUT, RANK, REPLICAS = 8192, 6144, 32, 8
TOK, FEAT, OWN = 1024, 512, 64
CW = 512
NC = D_OUT // CW
NT = (((1,), (1,)), ((), ()))

STAGE_AT = dict(a=1, b=3, c=5, d=7, e=9, f=9, g=10, h=11, i=12, j=13, k=14)
PARTS = 3
TILES = D_OUT // 128 * RANK // 8
PART = TILES // 2 // PARTS
STEPS = NC + 7
WIDE = 3072
EARLY = 3


def place():
    d, t = lax.axis_index("dp"), lax.axis_index("tensor")
    return dict(y_lo=d // 4, z=d % 4, x=t // 4, y_hi=(t // 2) % 2, core=t % 2)


def device(at, **moved):
    q = {**at, **moved}
    return {"dp": q["y_lo"] * 4 + q["z"], "tensor": q["x"] * 4 + q["y_hi"] * 2 + q["core"]}


def far_first(ring):
    return [(i, ring[i]) for i in (1, 0, 2)]


def along_y(at, by):
    y = (at["y_hi"] * 2 + at["y_lo"] + by) % 4
    return device(at, y_hi=y // 2, y_lo=y % 2)


def split3(v):
    hi = v.astype(BF16)
    rest = v - hi.astype(F32)
    mid = rest.astype(BF16)
    low = (rest - mid.astype(F32)).astype(BF16)
    return hi, mid, low


def rows3(v):
    return jnp.concatenate(split3(v), axis=0)


def sum3(v):
    n = v.shape[0] // 3
    return v[:n] + (v[n : 2 * n] + v[2 * n :])


def stack6(v):
    h, m, low = split3(v)
    return jnp.concatenate([h, m, h, low, h, m], axis=0)


def dot(a, b, dims=(((1,), (0,)), ((), ()))):
    return lax.dot_general(a, b, dims, preferred_element_type=F32)


def kernel(
    acts_hbm, grad_hbm, weight_hbm, residue_hbm, qt_hbm,
    gin_out, pt_ref, q_out, merged, i6, p6,
    g, pair_g, weight, residue, acts_t, gin, qt,
    qt3, gq_half, gq, gq3, part, ska_z, ska_y, skb_y, skb_z, st, st3, z_out, z_in, gram_in, gram_core, gram_all, linv,
    b_own, b_core, b_z, piece_z, b_y, b_x, q_all,
    load_sem, bulk_send, bulk_recv, core_send, core_recv, own_sem,
    gq_send, gq_recv, z_send, z_recv, gr_send, gr_recv, ring_send, ring_recv, pair_send, pair_recv,
    bc_send, bc_recv, rs_send, rs_recv, qc_send, qc_recv,
):
    acts = gin_out
    at = place()
    x, y_hi, y_lo, z, core = at["x"], at["y_hi"], at["y_lo"], at["z"], at["core"]
    y = y_hi * 2 + y_lo
    me = x * 4 + y_hi * 2 + core
    chip = x * 2 + y_hi
    other = device(at, core=1 - core)
    peers = [(2, 1), (1, 1), (3, 1), (2, 0), (0, 1), (1, 0), (3, 0)]
    peer_ids = [device(at, x=(x + dx) % 4, y_hi=(y_hi + dy) % 2) for dx, dy in peers]
    ring = {
        "x": [device(at, x=(x + i) % 4) for i in (1, 2, 3)],
        "y": [along_y(at, i) for i in (1, 2, 3)],
        "z": [device(at, z=(z + i) % 4) for i in (1, 2, 3)],
    }

    def chip_at(dx, dy):
        return ((x + dx + 4) % 4) * 2 + (y_hi + dy) % 2

    beyond, over = chip_at(2, 0), chip_at(0, 1)

    def chunk(k):
        return pl.ds(pl.multiple_of(k * CW, CW), CW)

    for k in range(NC):
        own = grad_hbm.at[:, pl.ds(k * CW, CW)]
        pltpu.make_async_copy(own, pair_g.at[k, core], load_sem.at[0]).start()
        pltpu.make_async_copy(own, g.at[k, chip, core], load_sem.at[5]).start()
    load_q = pltpu.make_async_copy(qt_hbm, qt, load_sem.at[1])
    load_res = pltpu.make_async_copy(residue_hbm, residue, load_sem.at[2])
    load_acts = pltpu.make_async_copy(acts_hbm, acts, load_sem.at[3])
    load_w = pltpu.make_async_copy(weight_hbm, weight, load_sem.at[4])
    load_q.start()
    load_acts.start()
    load_res.start()
    load_w.start()

    barrier = pltpu.get_barrier_semaphore()
    greet = [*peer_ids, other, ring["y"][0], ring["y"][2], *ring["z"]]
    for who in greet:
        pl.semaphore_signal(barrier, inc=1, device_id=who, device_id_type=MESH)
    load_q.wait()
    qt3[...] = rows3(qt[...])
    pltpu.make_async_copy(pair_g.at[:, core], pair_g.at[:, core], load_sem.at[0]).wait()
    pltpu.make_async_copy(g.at[:, chip, core], g.at[:, chip, core], load_sem.at[5]).wait()
    total = jnp.zeros((3 * RANK, 2 * OWN), F32)
    for k in range(NC):
        twice = jnp.concatenate([pair_g[k, core], pair_g[k, core]], axis=0)
        total += dot(qt3[:, k * CW : (k + 1) * CW], twice, NT)
    lane = lax.broadcasted_iota(jnp.int32, (RANK, 2 * OWN), 1)
    gq_half[core] = jnp.where(lane // OWN == core, sum3(total), 0.0)
    pl.semaphore_wait(barrier, len(greet))

    def remote(src, dst, send, recv, who):
        return pltpu.make_async_remote_copy(
            src_ref=src, dst_ref=dst, send_sem=send, recv_sem=recv, device_id=who, device_id_type=MESH
        )

    def bulk(flow, k, source, who):
        block = g.at[k, source, core]
        return remote(block, block, bulk_send.at[flow], bulk_recv.at[flow, k], who)

    def arrived(flow, k):
        bulk(flow, k, chip, other).wait_recv()

    def to_core(k):
        plane = g.at[k, :, core]
        return remote(plane, plane, core_send.at[0], core_recv.at[k], other)

    right, left, across = ring["x"][0], ring["x"][2], device(at, y_hi=1 - y_hi)

    own_copy = remote(pair_g.at[:, core], pair_g.at[:, core], own_sem.at[0], own_sem.at[1], other)
    half_copy = remote(gq_half.at[core], gq_half.at[core], own_sem.at[2], own_sem.at[3], other)
    half_copy.start()
    own_copy.start()

    def send_own(k):
        bulk(0, k, chip, right).start()
        bulk(1, k, chip, left).start()
        bulk(2, k, chip, across).start()

    def step(s, carry):
        @pl.when((s >= EARLY) & (s < NC))
        def _():
            send_own(s)

        @pl.when(s == 0)
        def _():
            send_own(0)
            half_copy.wait()
            gq[chip] = gq_half[0] + gq_half[1]
            for i, who in enumerate(peer_ids):
                remote(gq.at[chip], gq.at[chip], gq_send.at[i], gq_recv.at[i], who).start()
            for k in range(1, EARLY):
                send_own(k)
            load_res.wait()

            def add(k, total):
                return total + dot(qt3[:, chunk(k)], residue[:, chunk(k)], NT)

            part[...] = sum3(lax.fori_loop(0, NC, add, jnp.zeros((3 * RANK, FEAT), F32)))
            load_acts.wait()
            acts_t[...] = acts[...].T
            gin[...] = jnp.zeros_like(gin)

        @pl.when((s >= 2) & (s < NC + 2))
        def _():
            k = s - 2
            arrived(0, k)
            arrived(1, k)
            odd = k % 2
            ahead = device(at, x=(x + 1 + 2 * odd) % 4)
            bulk(3, k, chip_at(2 * odd - 1, 0), ahead).start()
            arrived(2, k)
            bulk(4, k, over, right).start()
            bulk(5, k, over, left).start()

        @pl.when((s >= 4) & (s < NC + 4))
        def _():
            k = s - 4
            arrived(3, k)
            bulk(6, k, beyond, across).start()
            arrived(4, k)
            arrived(5, k)

        @pl.when((s >= 6) & (s < NC + 6))
        def _():
            k = s - 6
            arrived(6, k)
            to_core(k).start()

        @pl.when(s == 4)
        def _():
            load_w.wait()

        @pl.when(s >= 7)
        def _():
            k = s - 7
            to_core(k).wait_recv()
            rows = g[k].reshape(TOK, CW)
            merged[k] = dot(acts_t[...], rows) + residue[:, chunk(k)].astype(F32)
            gin[...] += dot(rows, weight[:, chunk(k)], NT)

        def stage_at(name):
            return pl.when(s == STAGE_AT[name])

        def z_copies(ref, n):
            return [
                remote(ref.at[z], ref.at[z], ring_send.at[n, i], ring_recv.at[n, i], who)
                for i, who in far_first(ring["z"])
            ]

        def y_copy(ref, n):
            near = device(at, y_lo=1 - y_lo)
            return remote(ref.at[y_lo], ref.at[y_lo], pair_send.at[n], pair_recv.at[n], near)

        @stage_at("a")
        def _():
            for i, who in enumerate(peer_ids):
                remote(gq.at[chip], gq.at[chip], gq_send.at[i], gq_recv.at[i], who).wait()
            for j in range(8):
                gq3[:, j * 128 : (j + 1) * 128] = rows3(gq[j])
            sketch = part[...] + sum3(dot(gq3[...], acts[...]))
            ska_z[z] = sketch[:, : FEAT // 2]
            skb_y[y_lo] = sketch[:, FEAT // 2 :]
            y_copy(skb_y, 0).start()
            for c in z_copies(ska_z, 0):
                c.start()

        @stage_at("b")
        def _():
            y_copy(skb_y, 0).wait()
            skb_z[z] = skb_y[0] + skb_y[1]
            for c in z_copies(skb_z, 1):
                c.start()
            for c in z_copies(ska_z, 0):
                c.wait()
            ska_y[y_lo] = (ska_z[0] + ska_z[1]) + (ska_z[2] + ska_z[3])
            y_copy(ska_y, 1).start()

        @stage_at("c")
        def _():
            y_copy(ska_y, 1).wait()
            for c in z_copies(skb_z, 1):
                c.wait()
            low = ska_y[0] + ska_y[1]
            high = (skb_z[0] + skb_z[1]) + (skb_z[2] + skb_z[3])
            sketch = jnp.concatenate([low, high], axis=1) * (1.0 / REPLICAS)
            st[...] = sketch
            st3[...] = rows3(sketch)
            zt = sum3(dot(st3[...], acts_t[...]))
            for j in range(8):
                z_out[j] = zt[:, j * 128 : (j + 1) * 128]
            for i, who in enumerate(peer_ids):
                dx, dy = peers[i]
                there = ((x + dx) % 4) * 2 + (y_hi + dy) % 2
                remote(z_out.at[there], z_in.at[chip], z_send.at[i], z_recv.at[i], who).start()
            z_in[chip] = z_out[chip]
            gram = lax.dot_general(
                sketch, sketch, NT, precision=lax.Precision.HIGHEST, preferred_element_type=F32
            )
            for i in range(4):
                gram_in[chip, :, i * RANK : (i + 1) * RANK] = gram[i * 8 : (i + 1) * 8]
            for i, who in enumerate(peer_ids):
                remote(gram_in.at[chip], gram_in.at[chip], gr_send.at[i], gr_recv.at[i], who).start()

            def from_residue(k, _):
                r = sum3(dot(st3[...], residue[:, chunk(k)]))
                for i in range(CW // 128):
                    b_own[pl.ds(k * (CW // 32) + 4 * i, 4)] = r[:, i * 128 : (i + 1) * 128].reshape(4, 8, 128)
                return 0

            lax.fori_loop(0, NC, from_residue, 0)

        def tiles(c, h):
            return pl.ds(c * (TILES // 2) + h * PART, PART)

        def fourth(i):
            return pl.ds(i * (PART // 4), PART // 4)

        def core_copy(h, start):
            c = remote(b_own.at[tiles(1 - core, h)], b_core.at[h], bc_send.at[h], bc_recv.at[h], other)
            c.start() if start else c.wait()

        @stage_at("d")
        def _():
            for i, who in enumerate(peer_ids):
                remote(z_out.at[0], z_in.at[0], z_send.at[i], z_recv.at[i], who).wait()
            total = z_in[0]
            for j in range(1, 8):
                total = total + z_in[j]
            z3 = rows3(total)
            own_copy.wait_recv()

            def from_grad(k, _):
                r = sum3(dot(z3, pair_g[k].reshape(2 * OWN, CW)))
                for i in range(CW // 128):
                    b_own[pl.ds(k * (CW // 32) + 4 * i, 4)] += r[:, i * 128 : (i + 1) * 128].reshape(4, 8, 128)
                return 0

            each = NC // 2 // PARTS
            first = (1 - core) * (NC // 2)
            for h in range(PARTS):
                lax.fori_loop(first + h * each, first + (h + 1) * each, from_grad, 0)
                core_copy(h, True)
            lax.fori_loop(core * (NC // 2), (core + 1) * (NC // 2), from_grad, 0)
            for i, who in enumerate(peer_ids):
                remote(gram_in.at[chip], gram_in.at[chip], gr_send.at[i], gr_recv.at[i], who).wait()
            total = gram_in[0]
            for j in range(1, 8):
                total = total + gram_in[j]
            gram_core[core] = total
            remote(gram_core.at[core], gram_core.at[core], pair_send.at[2], pair_recv.at[2], other).start()

            for h in range(PARTS):
                core_copy(h, False)
                b_core[h] += b_own[tiles(core, h)]
                for i, who in far_first(ring["z"]):
                    there = fourth((z + i + 1) % 4)
                    remote(b_core.at[h, there], b_z.at[h, i], rs_send.at[0, h, i], rs_recv.at[0, h, i], who).start()
        @stage_at("e")
        def _():
            remote(gram_core.at[core], gram_core.at[core], pair_send.at[2], pair_recv.at[2], other).wait()
            packed = (gram_core[0] + gram_core[1]) * (1.0 / D_IN)
            gram_all[...] = jnp.zeros((RANK, 128), F32)
            for i in range(4):
                gram_all[i * 8 : (i + 1) * 8, 0:RANK] = packed[:, i * RANK : (i + 1) * RANK]
            sub = lax.broadcasted_iota(jnp.int32, (RANK, 128), 0)
            lane = lax.broadcasted_iota(jnp.int32, (RANK, 128), 1)
            unit = jnp.where(sub == lane, 1.0, 0.0).astype(F32)

            def eliminate(j, both):
                a, e = both
                row_a = jnp.sum(jnp.where(sub == j, a, 0.0), axis=0, keepdims=True)
                row_e = jnp.sum(jnp.where(sub == j, e, 0.0), axis=0, keepdims=True)
                col = jnp.sum(jnp.where(lane == j, a, 0.0), axis=1, keepdims=True)
                diag = jnp.sum(jnp.where(lane[0:1] == j, row_a, 0.0), axis=1, keepdims=True)
                scale = 1.0 / jnp.sqrt(diag)
                row_a, row_e = row_a * scale, row_e * scale
                factor = jnp.where(sub > j, col * scale, 0.0)
                a = jnp.where(sub == j, row_a, a - factor * row_a)
                e = jnp.where(sub == j, row_e, e - factor * row_e)
                return a, e

            linv[...] = lax.fori_loop(0, RANK, eliminate, (gram_all[...], unit))[1]
            ih, im, il = split3(linv[:, 0:RANK])
            i6[...] = jnp.concatenate([ih, ih, im, ih, il, im], axis=1)
            p_t = dot(i6[...], stack6(st[...]))
            pt_ref[...] = p_t
            ph, pm, pw = split3(p_t)
            p6[...] = jnp.concatenate([ph, ph, pm, ph, pw, pm], axis=0).T

        def landed_at(axis, stage, h, ref):
            for i, who in far_first(ring[axis]):
                remote(ref(i), ref(i), rs_send.at[stage, h, i], rs_recv.at[stage, h, i], who).wait()

        @stage_at("f")
        def _():
            for h in range(PARTS):
                landed_at("z", 0, h, lambda i: b_z.at[h, i])
                piece_z[h] = (b_core[h, fourth(z)] + b_z[h, 0]) + (b_z[h, 1] + b_z[h, 2])
                for i, who in far_first(ring["y"]):
                    there = pl.ds(((y + i + 1) % 4) * (PART // 16), PART // 16)
                    remote(piece_z.at[h, there], b_y.at[h, i], rs_send.at[1, h, i], rs_recv.at[1, h, i], who).start()

        @stage_at("g")
        def _():
            for h in range(PARTS):
                landed_at("y", 1, h, lambda i: b_y.at[h, i])
                own = piece_z[h, pl.ds(y * (PART // 16), PART // 16)]
                b_x[h, x] = (own + b_y[h, 0]) + (b_y[h, 1] + b_y[h, 2])
                for i, who in far_first(ring["x"]):
                    block = b_x.at[h, x]
                    remote(block, block, rs_send.at[2, h, i], rs_recv.at[2, h, i], who).start()

        def piece(h):
            return pl.ds(core * (TILES // 2) + h * PART + z * (PART // 4) + y * (PART // 16), PART // 16)

        def pieces(h):
            return pl.ds(core * (TILES // 2) + h * PART + z * (PART // 4), PART // 4)

        def last_copy(h):
            block = q_all.at[tiles(core, h)]
            return remote(block, block, qc_send.at[h], qc_recv.at[h], other)

        @stage_at("h")
        def _():
            for h in range(PARTS):
                landed_at("x", 2, h, lambda i: b_x.at[h, x])
                q_all[piece(h)] = (b_x[h, 0] + b_x[h, 1]) + (b_x[h, 2] + b_x[h, 3])
                for i, who in far_first(ring["y"]):
                    block = q_all.at[piece(h)]
                    remote(block, block, rs_send.at[3, h, i], rs_recv.at[3, h, i], who).start()

        @stage_at("i")
        def _():
            for h in range(PARTS):
                landed_at("y", 3, h, lambda i: q_all.at[piece(h)])
                for i, who in far_first(ring["z"]):
                    block = q_all.at[pieces(h)]
                    remote(block, block, rs_send.at[4, h, i], rs_recv.at[4, h, i], who).start()

        @stage_at("j")
        def _():
            for h in range(PARTS):
                landed_at("z", 4, h, lambda i: q_all.at[pieces(h)])
                last_copy(h).start()

        @stage_at("k")
        def _():
            for h in range(PARTS):
                last_copy(h).wait()

        return carry

    lax.fori_loop(0, STEPS, step, 0)

    q_out[...] = q_all[...]
    gin_out[...] = gin[...].astype(BF16)

    own_copy.wait_send()
    for flow in range(7):
        block = g.at[:, 0, 0]
        remote(block, block, bulk_send.at[flow], bulk_recv.at[flow, 0], other).wait_send()
    block = g.at[:, :, core]
    remote(block, block, core_send.at[0], core_recv.at[0], other).wait_send()


def finish(
    gin, p_t, q_all, merged, i6, p6, gin_hbm, pt_hbm, qt_hbm, new_hbm, new, q_t, b_t, q6, sem
):
    store_gin = pltpu.make_async_copy(gin, gin_hbm, sem.at[0])
    store_p = pltpu.make_async_copy(p_t, pt_hbm, sem.at[1])
    store_gin.start()
    store_p.start()

    def right(j, carry):
        columns = pl.ds(pl.multiple_of(j * WIDE, WIDE), WIDE)
        for i in range(WIDE // 128):
            block = q_all[pl.ds(j * (WIDE // 32) + 4 * i, 4)]
            b_t[:, i * 128 : (i + 1) * 128] = block.reshape(RANK, 128)
        q = dot(i6[...], stack6(b_t[...])) * (1.0 / (REPLICAS * math.sqrt(D_IN)))
        q_t[:, columns] = q
        q6[:, columns] = stack6(q * (1.0 / math.sqrt(D_IN)))
        return carry

    def body(k, carry):
        columns = pl.ds(pl.multiple_of(k * CW, CW), CW)
        new[k] = (merged[k] - dot(p6[...], q6[:, columns])).astype(BF16)
        pltpu.make_async_copy(new.at[k], new_hbm.at[:, columns], sem.at[2]).start()
        return carry

    lax.fori_loop(0, D_OUT // WIDE, right, 0)
    store_q = pltpu.make_async_copy(q_t, qt_hbm, sem.at[3])
    store_q.start()
    lax.fori_loop(0, NC, body, 0, unroll=3)
    pltpu.make_async_copy(new, new, sem.at[2]).wait()
    store_gin.wait()
    store_p.wait()
    store_q.wait()


def shards(acts, grad_out, weight, residue, start_q):
    vmem, dma = pltpu.VMEM, pltpu.SemaphoreType.DMA
    hbm = pl.BlockSpec(memory_space=pl.ANY)
    here = pl.BlockSpec(memory_space=pltpu.VMEM)
    flops = 4 * TOK * FEAT * D_OUT
    results = pl.pallas_call(
        kernel,
        out_shape=[
            vmem((TOK, FEAT), BF16),
            vmem((RANK, FEAT), F32),
            vmem((TILES, 8, 128), F32),
            vmem((NC, FEAT, CW), F32),
            vmem((RANK, 6 * RANK), BF16),
            vmem((FEAT, 6 * RANK), BF16),
        ],
        in_specs=[hbm] * 5,
        out_specs=[here] * 6,
        scratch_shapes=[
            vmem((NC, TOK // OWN // 2, 2, OWN, CW), BF16),
            vmem((NC, 2, OWN, CW), BF16),
            vmem((FEAT, D_OUT), BF16),
            vmem((FEAT, D_OUT), BF16),
            vmem((FEAT, TOK), BF16),
            vmem((TOK, FEAT), F32),
            vmem((RANK, D_OUT), F32),
            vmem((3 * RANK, D_OUT), BF16),
            vmem((2, RANK, 128), F32),
            vmem((8, RANK, 128), F32),
            vmem((3 * RANK, TOK), BF16),
            vmem((RANK, FEAT), F32),
            vmem((4, RANK, FEAT // 2), F32),
            vmem((2, RANK, FEAT // 2), F32),
            vmem((2, RANK, FEAT // 2), F32),
            vmem((4, RANK, FEAT // 2), F32),
            vmem((RANK, FEAT), F32),
            vmem((3 * RANK, FEAT), BF16),
            vmem((8, RANK, 128), F32),
            vmem((8, RANK, 128), F32),
            vmem((8, 8, 128), F32),
            vmem((2, 8, 128), F32),
            vmem((RANK, 128), F32),
            vmem((RANK, 128), F32),
            vmem((TILES, 8, 128), F32),
            vmem((PARTS, PART, 8, 128), F32),
            vmem((PARTS, 3, PART // 4, 8, 128), F32),
            vmem((PARTS, PART // 4, 8, 128), F32),
            vmem((PARTS, 3, PART // 16, 8, 128), F32),
            vmem((PARTS, 4, PART // 16, 8, 128), F32),
            vmem((TILES, 8, 128), F32),
            dma((6,)),
            dma((7,)),
            dma((7, NC)),
            dma((1,)),
            dma((NC,)),
            dma((4,)),
            dma((7,)),
            dma((7,)),
            dma((7,)),
            dma((7,)),
            dma((7,)),
            dma((7,)),
            dma((2, 3)),
            dma((2, 3)),
            dma((3,)),
            dma((3,)),
            dma((PARTS,)),
            dma((PARTS,)),
            dma((5, PARTS, 3)),
            dma((5, PARTS, 3)),
            dma((PARTS,)),
            dma((PARTS,)),
        ],
        compiler_params=pltpu.CompilerParams(
            collective_id=1, has_side_effects=True, vmem_limit_bytes=40 * 2**20
        ),
        cost_estimate=pl.CostEstimate(flops=flops, bytes_accessed=24 * 2**20, transcendentals=0),
        name="gather_and_compress",
    )(*(pltpu.with_memory_space_constraint(a, pltpu.HBM) for a in (acts, grad_out, weight, residue[0], start_q.T)))
    grad_in, p_t, q_t, new = pl.pallas_call(
        finish,
        out_shape=[
            jax.ShapeDtypeStruct((TOK, FEAT), BF16),
            jax.ShapeDtypeStruct((RANK, FEAT), F32),
            jax.ShapeDtypeStruct((RANK, D_OUT), F32),
            jax.ShapeDtypeStruct((FEAT, D_OUT), BF16),
        ],
        in_specs=[here] * 6,
        out_specs=[hbm] * 4,
        scratch_shapes=[
            vmem((NC, FEAT, CW), BF16),
            vmem((RANK, D_OUT), F32),
            vmem((RANK, WIDE), F32),
            vmem((6 * RANK, D_OUT), BF16),
            dma((4,)),
        ],
        compiler_params=pltpu.CompilerParams(vmem_limit_bytes=14 * 2**20),
        name="finish",
    )(*(pltpu.with_memory_space_constraint(r, pltpu.VMEM) for r in results))
    return grad_in, p_t.T, q_t.T, new[None]


def solution(mesh):
    in_specs = (
        P("dp", "tensor"),
        P(("dp", "tensor"), None),
        P("tensor", None),
        P("dp", "tensor", None),
        P(),
    )
    out_specs = (P("dp", "tensor"), P("tensor", None), P(), P("dp", "tensor", None))
    return jax.shard_map(shards, mesh=mesh, in_specs=in_specs, out_specs=out_specs, check_vma=False)
```
